32 devices in a mesh: node: 8 (over z, y), local: 4 (over x, core).
Axes of the slice: x: 2, y: 2, z: 4, core: 2. Of those that a mesh axis runs over, the one named last changes fastest.
Arguments:
- hidden: bfloat16 [4096, 3584], P(('node', 'local')), may hold values from -6 to 6
- latent_weight: bfloat16 [3584, 576], P('node'), may hold values from -0.09375 to 0.09375
- latent_gain: float32 [512], replicated, may hold values from 0.1 to 1.9
- queries: bfloat16 [4096, 12288], P(('node', 'local')), may hold values from -200 to 200
- kv_weight: bfloat16 [512, 16384], P('node', 'local'), may hold values from -0.25 to 0.25
- expert_ids: int32 [4096, 8], P(('node', 'local')), may hold values from 0 to 255, as said below
- route_weights: float32 [4096, 8], P(('node', 'local')), may hold values from 0.05 to 0.6
- gate_proj: bfloat16 [32, 3584, 512], P(('node', 'local')), may hold values from -0.09375 to 0.09375
- up_proj: bfloat16 [32, 3584, 512], P(('node', 'local')), may hold values from -0.09375 to 0.09375
- down_proj: bfloat16 [32, 512, 3584], P(('node', 'local')), may hold values from -0.1875 to 0.1875
Outputs:
- attention: bfloat16 [4096, 8192], P(('node', 'local'))
- routed: bfloat16 [4096, 3584], P(('node', 'local'))
The draws below stay inside these ranges and needn't reach their ends.
Inputs may be any that keep to these rules, and one draw needn't show every extreme that they name: `expert_ids`: each row names 8 different experts, all of them in at most 4 of the 8 groups of 32 consecutive expert numbers.
All inputs are finite; a program needn't handle non-finite values.
Results may differ from the reference program's by a relative error of at most 0.014.
The reference program's roundings to bfloat16 on the way count: a program that leaves them out, or rounds other values in their place, can miss the bound.
Values may be sent and summed in bfloat16 or wider, within the bound.
A program may use at most 128 MiB of HBM per device.

```python
import math
import jax
import jax.numpy as jnp
from jax import lax

D = 3584
HEADS = 64
NOPE = 128
ROPE = 64
VDIM = 128
LAT = 512
EXPERTS = 256
GROUPS = 8
TOPK = 8
FF_E = 1024
TOK_DEV = 128
L = 512
TOKENS = 4096
FLIGHT = 16
STRIDE = 16
CAP = 8
N_NODE = 8
N_LOCAL = 4


def draw_queries(key, part):
    key = jax.random.fold_in(key, 11)
    shape = (TOKENS, HEADS * (NOPE + ROPE))
    return jax.random.normal(key, shape, jnp.float32).astype(jnp.bfloat16)


def draw_expert_ids(key, part):
    key = jax.random.fold_in(key, 5)
    group_key, bias_key, expert_key, pick_key = jax.random.split(key, 4)
    per_group = EXPERTS // GROUPS
    group_bias = jax.random.randint(bias_key, (GROUPS,), 0, 4) * 32768
    group_scores = jax.random.randint(group_key, (TOKENS, GROUPS), 0, 65536) + group_bias[None, :]
    group_scores = group_scores * GROUPS + jnp.arange(GROUPS, dtype=jnp.int32)[None, :]
    chosen = lax.top_k(group_scores, 4)[1]
    expert_group = jnp.arange(EXPERTS, dtype=jnp.int32) // per_group
    allowed = jnp.any(chosen[:, :, None] == expert_group[None, None, :], axis=1)
    popularity = jax.random.randint(expert_key, (EXPERTS,), 0, 8)
    popularity = popularity * popularity * 2048
    scores = jax.random.randint(pick_key, (TOKENS, EXPERTS), 0, 65536) + popularity[None, :]
    scores = jnp.where(allowed, scores, -1) * EXPERTS + jnp.arange(EXPERTS, dtype=jnp.int32)[None, :]
    return lax.top_k(scores, TOPK)[1].astype(jnp.int32)


def steps_of(rng, shape, pieces, least, top_value):
    factor_of, own = 1.0, jax.random.fold_in(rng, 6)
    for axis_at, blocks in pieces:
        steps = jnp.exp(jax.random.uniform(jax.random.fold_in(own, axis_at), (blocks,), jnp.float32, least / len(pieces), top_value / len(pieces)))
        factor_of = factor_of * jnp.repeat(steps, shape[axis_at] // blocks).reshape([-1 if axis == axis_at else 1 for axis in range(len(shape))])
    return factor_of


def centred(key, extent, deviation, reach, pieces=(), held_as=jnp.bfloat16):
    loudness = steps_of(key, extent, pieces, -0.22, 0.18) if pieces else 1.0
    entries = jax.random.normal(key, extent, jnp.float32) * deviation * loudness
    return jnp.minimum(jnp.maximum(entries, -reach), reach).astype(held_as)


def setup_inputs(seed: int = 0) -> dict:
    arg_keys = jax.random.split(jax.random.key(seed), 11)
    hidden = centred(arg_keys[0], (TOKENS, D), 1.0, 6.0, ((0, 32),))
    latent_weight = centred(arg_keys[1], (D, LAT + ROPE), D ** -0.5, 0.09375, ((0, 8),))
    latent_gain = jnp.clip(1.0 + 0.18 * jax.random.normal(arg_keys[2], (LAT,), jnp.float32), 0.1, 1.9)
    queries = draw_queries(jax.random.fold_in(arg_keys[10], 71), 0)
    kv_weight = centred(arg_keys[4], (LAT, HEADS * (NOPE + VDIM)), LAT ** -0.5, 0.25, ((0, 8), (1, 4)))
    expert_ids = draw_expert_ids(jax.random.fold_in(arg_keys[10], 71), 0)
    route_weights = jnp.clip(0.05 + 0.55 * jax.random.uniform(arg_keys[6], (TOKENS, TOPK), jnp.float32) ** steps_of(arg_keys[6], (TOKENS, TOPK), ((0, 32),), -0.2, 0.2), 0.05, 0.6)
    gate_proj = centred(arg_keys[7], (2 * FLIGHT, D, FF_E // 2), D ** -0.5, 0.09375, ((0, 32),))
    up_proj = centred(arg_keys[8], (2 * FLIGHT, D, FF_E // 2), D ** -0.5, 0.09375, ((0, 32),))
    down_proj = centred(arg_keys[9], (2 * FLIGHT, FF_E // 2, D), FF_E ** -0.5, 0.1875, ((0, 32),))
    return dict(hidden=hidden, latent_weight=latent_weight, latent_gain=latent_gain, queries=queries, kv_weight=kv_weight, expert_ids=expert_ids, route_weights=route_weights, gate_proj=gate_proj, up_proj=up_proj, down_proj=down_proj)


def normalize(columns, latent_gain):
    mean_square = lax.optimization_barrier(jnp.mean(columns * columns, axis=1, keepdims=True))
    return (columns * lax.rsqrt(mean_square + 1e-06) * latent_gain[None, :]).astype(jnp.bfloat16)

def rotate_keys(rope_part, position):
    half_width = ROPE // 2
    freqs = 10000.0 ** (-2.0 * jnp.arange(half_width, dtype=jnp.float32) / ROPE)
    angles = position.astype(jnp.float32)[:, None] * freqs[None, :]
    cosine = jnp.cos(angles)
    sine = jnp.sin(angles)
    first_half = rope_part[:, :half_width]
    second_half = rope_part[:, half_width:]
    return jnp.concatenate([first_half * cosine - second_half * sine, second_half * cosine + first_half * sine], axis=1)

def attend_head(query_rows, keyval, keys_rope):
    length = query_rows.shape[0]
    q_block = min(length, 512)
    keys_nope = keyval[:, :NOPE]
    values = keyval[:, NOPE:]
    scale = 1.0 / math.sqrt(NOPE + ROPE)

    def one_block(block_index):
        offset = block_index * q_block
        block_rows = lax.dynamic_slice_in_dim(query_rows, offset, q_block, 0)
        scores = jnp.dot(block_rows[:, :NOPE], keys_nope.T, preferred_element_type=jnp.float32)
        scores = scores + jnp.dot(block_rows[:, NOPE:], keys_rope.T, preferred_element_type=jnp.float32)
        scores = scores * scale
        query_pos = offset + jnp.arange(q_block, dtype=jnp.int32)[:, None]
        key_pos = jnp.arange(length, dtype=jnp.int32)[None, :]
        scores = jnp.where(key_pos <= query_pos, scores, -1e+30)
        row_max = lax.optimization_barrier(jnp.max(scores, axis=1, keepdims=True))
        weights = jnp.exp(scores - row_max)
        probs = (weights / lax.optimization_barrier(jnp.sum(weights, axis=1, keepdims=True))).astype(jnp.bfloat16)
        return jnp.dot(probs, values, preferred_element_type=jnp.float32).astype(jnp.bfloat16)
    blocks = lax.map(one_block, jnp.arange(length // q_block, dtype=jnp.int32))
    return blocks.reshape(length, values.shape[1])

def reference(hidden, latent_weight, latent_gain, queries, kv_weight, expert_ids, route_weights, gate_proj, up_proj, down_proj):
    latent = jnp.dot(hidden, latent_weight, preferred_element_type=jnp.float32)
    compressed = normalize(latent[:, :LAT], latent_gain)
    position = jnp.arange(TOKENS, dtype=jnp.int32) % L
    rope_keys = rotate_keys(latent[:, LAT:], position).astype(jnp.bfloat16)

    def one_sequence(packed):
        seq_queries, seq_latent, seq_rope = packed
        keyval = jnp.dot(seq_latent, kv_weight, preferred_element_type=jnp.float32).astype(jnp.bfloat16)
        head_queries = seq_queries.reshape(L, HEADS, NOPE + ROPE).transpose(1, 0, 2)
        head_keyval = keyval.reshape(L, HEADS, NOPE + VDIM).transpose(1, 0, 2)
        outputs = lax.map(lambda head_pair: attend_head(head_pair[0], head_pair[1], seq_rope), (head_queries, head_keyval))
        return outputs.transpose(1, 0, 2).reshape(L, HEADS * VDIM)
    sequences = TOKENS // L
    attention = lax.map(one_sequence, (queries.reshape(sequences, L, HEADS * (NOPE + ROPE)), compressed.reshape(sequences, L, LAT), rope_keys.reshape(sequences, L, ROPE)))
    attention = attention.reshape(TOKENS, HEADS * VDIM)
    devices = N_NODE * N_LOCAL
    routes_flat = expert_ids.reshape(devices, TOK_DEV * TOPK)
    in_flight = routes_flat % STRIDE == 0
    target = routes_flat // STRIDE
    onehot = ((target[:, :, None] == jnp.arange(FLIGHT, dtype=jnp.int32)[None, None, :]) & in_flight[:, :, None]).astype(jnp.int32)
    slot_index = lax.optimization_barrier(jnp.sum((jnp.cumsum(onehot, axis=1) - onehot) * onehot, axis=2))
    kept_mask = in_flight & (slot_index < CAP)
    block_ids = jnp.arange(devices, dtype=jnp.int32)[:, None]
    dump_slot = FLIGHT * devices * CAP
    place_index = jnp.where(kept_mask, target * (devices * CAP) + block_ids * CAP + slot_index, dump_slot)
    token_index = block_ids * TOK_DEV + jnp.arange(TOK_DEV * TOPK, dtype=jnp.int32)[None, :] // TOPK
    row_table = jnp.full((dump_slot + 1,), TOKENS, jnp.int32).at[place_index.reshape(-1)].set(token_index.reshape(-1))[:dump_slot]
    padded = jnp.concatenate([hidden, jnp.zeros((1, D), jnp.bfloat16)], axis=0)
    half_width = FF_E // 2

    def run_expert(packed):
        expert_table, gates, ups, downs = packed
        row_block = padded[expert_table]
        halves = []
        for core_half in range(2):
            gate = jnp.dot(row_block, gates[core_half], preferred_element_type=jnp.float32)
            upper = jnp.dot(row_block, ups[core_half], preferred_element_type=jnp.float32)
            inner = (jax.nn.silu(gate) * upper).astype(jnp.bfloat16)
            halves.append(jnp.dot(inner, downs[core_half], preferred_element_type=jnp.float32).astype(jnp.bfloat16))
        return (halves[0].astype(jnp.float32) + halves[1].astype(jnp.float32)).astype(jnp.bfloat16)
    results = lax.map(run_expert, (row_table.reshape(FLIGHT, devices * CAP), gate_proj.reshape(FLIGHT, 2, D, half_width), up_proj.reshape(FLIGHT, 2, D, half_width), down_proj.reshape(FLIGHT, 2, half_width, D)))
    results = jnp.concatenate([results.reshape(FLIGHT * devices * CAP, D), jnp.zeros((1, D), jnp.bfloat16)], axis=0)
    route_index = place_index.reshape(TOKENS, TOPK)
    routed = jnp.zeros((TOKENS, D), jnp.float32)
    for column in range(TOPK):
        routed = routed + route_weights[:, column:column + 1] * results[route_index[:, column]].astype(jnp.float32)
    return (attention, routed.astype(jnp.bfloat16))
```

```python
import functools
import math

import jax
import jax.numpy as jnp
from jax import lax
from jax.experimental import pallas as pl
from jax.experimental.pallas import tpu as pltpu
from jax.sharding import PartitionSpec as P

NOPE = 128
ROPE = 64
VDIM = 128
LAT = 512
EXPERTS = 256
CAP = 8
PAIR_Q = 2 * (NOPE + ROPE)
PAIR_KV = 2 * (NOPE + VDIM)
PAIR_V = 2 * VDIM
MESH = pl.DeviceIdType.MESH
VMEM_LIMIT = 56 * 2**20


def remote(src, dst, send_sem, recv_sem, device):
    return pltpu.make_async_remote_copy(
        src_ref=src,
        dst_ref=dst,
        send_sem=send_sem,
        recv_sem=recv_sem,
        device_id=device,
        device_id_type=MESH,
    )


def greet(devices, n_local, me):
    barrier = pltpu.get_barrier_semaphore()

    def signal(d, carry):
        other = lax.rem(me + d, devices)
        pl.semaphore_signal(
            barrier,
            inc=1,
            device_id=(lax.div(other, n_local), lax.rem(other, n_local)),
            device_id_type=MESH,
        )
        return carry

    lax.fori_loop(1, devices, signal, 0)
    pl.semaphore_wait(barrier, devices - 1)


class Gather:
    def __init__(self, own, slot, nz, ny, node, local, sems):
        self.own, self.slot, self.nz, self.ny = own, slot, nz, ny
        self.z, self.y, self.local = lax.div(node, ny), lax.rem(node, ny), local
        self.up_s, self.up_r, self.dn_s, self.dn_r, self.y_s, self.y_r = sems

    def up(self, h, src):
        z = jnp.maximum(self.z - h, 0)
        dst = self.slot(z * self.ny + self.y)
        to = jnp.minimum(self.z + 1, self.nz - 1)
        return remote(
            dst if src is None else src, dst, self.up_s.at[h], self.up_r.at[h], (to * self.ny + self.y, self.local)
        )

    def down(self, h, src):
        z = jnp.minimum(self.z + h, self.nz - 1)
        dst = self.slot(z * self.ny + self.y)
        to = jnp.maximum(self.z - 1, 0)
        return remote(
            dst if src is None else src, dst, self.dn_s.at[h], self.dn_r.at[h], (to * self.ny + self.y, self.local)
        )

    def across(self, z, dy, src):
        dst = self.slot(z * self.ny + self.y)
        to = self.z * self.ny + lax.rem(self.y + dy, self.ny)
        return remote(
            dst if src is None else src, dst, self.y_s.at[z, dy - 1], self.y_r.at[z, dy - 1], (to, self.local)
        )

    def begin(self):
        @pl.when(self.z < self.nz - 1)
        def _():
            self.up(0, self.own).start()

        @pl.when(self.z > 0)
        def _():
            self.down(0, self.own).start()

        for dy in range(1, self.ny):
            self.across(self.z, dy, self.own).start()

    def hop(self, h, landed=None):
        @pl.when(self.z - h >= 0)
        def _():
            self.up(h - 1, None).wait_recv()
            if h < self.nz - 1:

                @pl.when(self.z < self.nz - 1)
                def _():
                    self.up(h, None).start()

            for dy in range(1, self.ny):
                self.across(self.z - h, dy, None).start()
            if landed:
                landed((self.z - h) * self.ny + self.y)

        @pl.when(self.z + h < self.nz)
        def _():
            self.down(h - 1, None).wait_recv()
            if h < self.nz - 1:

                @pl.when(self.z > 0)
                def _():
                    self.down(h, None).start()

            for dy in range(1, self.ny):
                self.across(self.z + h, dy, None).start()
            if landed:
                landed((self.z + h) * self.ny + self.y)

    def columns(self, landed=None):
        for z in range(self.nz):
            for dy in range(1, self.ny):
                self.across(z, dy, None).wait_recv()
                if landed:
                    landed(z * self.ny + lax.rem(self.y - dy + self.ny, self.ny))

    def finish(self):
        for h in range(self.nz - 1):

            @pl.when((self.z < self.nz - 1) & (self.z - h >= 0))
            def _():
                self.up(h, None).wait_send()

            @pl.when((self.z > 0) & (self.z + h < self.nz))
            def _():
                self.down(h, None).wait_send()

        for z in range(self.nz):
            for dy in range(1, self.ny):
                self.across(z, dy, None).wait_send()


def first_kernel(
    n_node,
    n_local,
    nz,
    hidden,
    pick,
    gain,
    cosine,
    sine,
    latent_w,
    queries,
    kv_w,
    gate_w,
    up_w,
    down_w,
    seq_out,
    q_out,
    kv_out,
    returned,
    lat,
    gates,
    ups,
    downs,
    leaving,
    arrived,
    part,
    sibpart,
    mine,
    local_sem,
    lat_sems,
    kv_sems,
    core_s,
    core_r,
    q_s,
    q_r,
    seq_s,
    seq_r,
    go_s,
    go_r,
    back_s,
    back_r,
    sib_s,
    sib_r,
):
    node, local = lax.axis_index("node"), lax.axis_index("local")
    devices, ny = n_node * n_local, n_node // nz
    chips = devices // 2
    me = node * n_local + local
    chip, core = lax.div(me, 2), lax.rem(me, 2)
    sibling = (node, local + 1 - 2 * core)
    half = lat.shape[2]
    tokens = hidden.shape[0]
    q_cols = q_out.shape[2]

    own_q = pl.ds(pl.multiple_of(local * q_cols, 128), q_cols)
    locals_ = [
        pltpu.make_async_copy(gate_w.at[0], gates, local_sem.at[0]),
        pltpu.make_async_copy(up_w.at[0], ups, local_sem.at[1]),
        pltpu.make_async_copy(down_w.at[0], downs, local_sem.at[2]),
        pltpu.make_async_copy(kv_w, kv_out.at[node], local_sem.at[3]),
        pltpu.make_async_copy(queries.at[:, own_q], q_out.at[local], local_sem.at[4]),
        pltpu.make_async_copy(latent_w.at[pl.ds(0, half)], lat.at[node, 0], local_sem.at[5]),
        pltpu.make_async_copy(latent_w.at[pl.ds(half, half)], lat.at[node, 1], local_sem.at[6]),
    ]
    for copy in locals_:
        copy.start()

    rows = jnp.dot(pick[...], hidden[...], preferred_element_type=jnp.float32)
    leaving[...] = rows.reshape(leaving.shape).astype(jnp.bfloat16)
    arrived[core, chip] = leaving[chip]

    greet(devices, n_local, me)

    def device_of(c):
        dev = c * 2 + core
        return (lax.div(dev, n_local), lax.rem(dev, n_local))

    def go(d):
        to = lax.rem(chip + d, chips)
        return remote(
            leaving.at[to], arrived.at[core, chip], go_s.at[d - 1], go_r.at[d - 1], device_of(to)
        )

    def back(d):
        to = lax.rem(chip + d, chips)
        return remote(
            part.at[core, to], returned.at[chip], back_s.at[d - 1], back_r.at[d - 1], device_of(to)
        )

    def each(first, last, act):
        def step(d, carry):
            act(d)
            return carry

        lax.fori_loop(first, last, step, 0)

    def ask(d):
        to = lax.rem(local + d, n_local)
        cols = pl.ds(pl.multiple_of(to * q_cols, 128), q_cols)
        return remote(
            queries.at[:, cols], q_out.at[local], q_s.at[d - 1], q_r.at[d - 1], (node, to)
        )

    lat_gather = Gather(
        latent_w.at[pl.ds(pl.multiple_of(core * half, 16), half)],
        lambda n: lat.at[n, core],
        nz,
        ny,
        node,
        local,
        lat_sems,
    )
    kv_gather = Gather(kv_w, lambda n: kv_out.at[n], nz, ny, node, local, kv_sems)

    def share(n):
        return remote(lat.at[n, core], lat.at[n, core], core_s.at[n], core_r.at[n], sibling)

    lat_gather.begin()
    each(1, chips, lambda d: go(d).start())
    kv_gather.begin()
    for d in range(1, n_local):
        ask(d).start()

    def landed(n):
        share(n).start()

    lat_gather.hop(1, landed)
    kv_gather.hop(1)
    lat_gather.hop(2, landed) if nz > 2 else None

    each(1, chips, lambda d: go(d).wait_recv())
    swap = remote(arrived.at[core], arrived.at[core], sib_s.at[0], sib_r.at[0], sibling)
    swap.start()
    for h in range(3, nz):
        lat_gather.hop(h, landed)
    if nz > 2:
        kv_gather.hop(2)
    for copy in locals_:
        copy.wait()
    swap.wait()

    block = 32
    per = chips // block if chips >= block else 1
    step_chips = min(block, chips)

    def expert(i, carry):
        c, p = lax.div(i, per), lax.rem(i, per)
        at = pl.ds(p * step_chips, step_chips)
        x = arrived[c, at].astype(jnp.float32).reshape(step_chips * CAP, -1).astype(jnp.bfloat16)
        gate = jnp.dot(x, gates[...], preferred_element_type=jnp.float32)
        upper = jnp.dot(x, ups[...], preferred_element_type=jnp.float32)
        inner = (gate / (1.0 + jnp.exp(-gate)) * upper).astype(jnp.bfloat16)
        width = downs.shape[1] // 7
        for j in range(7):
            cols = slice(j * width, (j + 1) * width)
            y = jnp.dot(inner, downs[:, cols], preferred_element_type=jnp.float32)
            part[c, at, :, cols] = y.reshape(step_chips, CAP, width).astype(jnp.bfloat16)
        return carry

    lax.fori_loop(0, 2 * per, expert, 0)
    give = remote(part.at[1 - core], sibpart, sib_s.at[1], sib_r.at[1], sibling)
    give.start()
    lat_gather.columns(landed)
    for h in range(3, nz):
        kv_gather.hop(h)
    give.wait()

    def total(p, carry):
        both = part[core, p].astype(jnp.float32) + sibpart[p].astype(jnp.float32)
        part[core, p] = both.astype(jnp.bfloat16)
        return carry

    lax.fori_loop(0, chips, total, 0)
    each(1, chips, lambda d: back(d).start())
    kept = pltpu.make_async_copy(part.at[core, chip], returned.at[chip], local_sem.at[7])
    kept.start()

    def other_half(n):
        return remote(
            lat.at[n, 1 - core], lat.at[n, 1 - core], core_s.at[n], core_r.at[n], sibling
        )

    def shared(n, carry):
        @pl.when(n != node)
        def _():
            other_half(n).wait_recv()

        return carry

    lax.fori_loop(0, n_node, shared, 0)
    weight = lat[...].reshape(n_node * 2 * half, lat.shape[3])
    latent = jnp.dot(hidden[...], weight, preferred_element_type=jnp.float32)
    u = latent[:, :LAT]
    scale = lax.rsqrt(jnp.mean(u * u, axis=1, keepdims=True) + 1e-06)
    mine[:, :LAT] = (u * scale * gain[...]).astype(jnp.bfloat16)
    a = latent[:, LAT:]
    swapped = jnp.concatenate([a[:, ROPE // 2 :], a[:, : ROPE // 2]], axis=1)
    mine[:, LAT:] = (a * cosine[...] + swapped * sine[...]).astype(jnp.bfloat16)

    def tell(d):
        to = lax.rem(local + d, n_local)
        return remote(mine, seq_out.at[local], seq_s.at[d - 1], seq_r.at[d - 1], (node, to))

    for d in range(1, n_local):
        tell(d).start()
    stays = pltpu.make_async_copy(mine, seq_out.at[local], local_sem.at[8])
    stays.start()

    kv_gather.columns()
    for d in range(1, n_local):
        ask(d).wait()
        tell(d).wait()
    each(1, chips, lambda d: back(d).wait())
    each(1, chips, lambda d: go(d).wait_send())
    kept.wait()
    stays.wait()
    lat_gather.finish()
    kv_gather.finish()

    def shared_sent(n, carry):
        @pl.when(n != node)
        def _():
            share(n).wait_send()

        return carry

    lax.fori_loop(0, n_node, shared_sent, 0)


def second_kernel(
    n_node, n_local, seq, queries, kv, results, combine, attention, routed, outs, send, recv, keep
):
    node, local = lax.axis_index("node"), lax.axis_index("local")
    devices = n_node * n_local
    me = node * n_local + local
    length = seq.shape[0]
    tokens = length // n_local
    pairs = kv.shape[1] // PAIR_KV
    wide = kv.shape[1] // 2
    scale = 1.0 / math.sqrt(NOPE + ROPE)
    step = 256

    barrier = pltpu.get_barrier_semaphore()
    for d in range(1, n_local):
        pl.semaphore_signal(
            barrier,
            inc=1,
            device_id=(node, lax.rem(local + d, n_local)),
            device_id_type=MESH,
        )

    def place(p):
        return pl.ds(pl.multiple_of(local * wide + p * PAIR_V, 128), PAIR_V)

    def tell(p, d):
        to = lax.rem(local + d, n_local)
        rows = pl.ds(pl.multiple_of(to * tokens, 16), tokens)
        return remote(
            outs.at[rows, pl.ds(pl.multiple_of(p * PAIR_V, 128), PAIR_V)],
            attention.at[:, place(p)],
            send.at[p, d - 1],
            recv.at[p, d - 1],
            (node, to),
        )

    def own(p):
        rows = pl.ds(pl.multiple_of(local * tokens, 16), tokens)
        return pltpu.make_async_copy(
            outs.at[rows, pl.ds(pl.multiple_of(p * PAIR_V, 128), PAIR_V)],
            attention.at[:, place(p)],
            keep.at[p],
        )

    compressed = seq[:, :LAT]
    rope = seq[:, LAT:].astype(jnp.float32)
    zeros = jnp.zeros((length, 128 - ROPE), jnp.float32)
    diagonal = lax.broadcasted_iota(jnp.int32, (step, step), 1) <= lax.broadcasted_iota(
        jnp.int32, (step, step), 0
    )

    def pair(p, carry):
        cols = pl.ds(pl.multiple_of(p * PAIR_KV, 128), PAIR_KV)
        keyval = jnp.dot(compressed, kv[:, cols], preferred_element_type=jnp.float32)
        first = jnp.concatenate([keyval[:, :NOPE], rope, zeros], axis=1).astype(jnp.bfloat16)
        at = NOPE + VDIM
        second = jnp.concatenate([zeros, keyval[:, at : at + NOPE], rope], axis=1).astype(
            jnp.bfloat16
        )
        for h, keys in enumerate((first, second)):
            values = keyval[:, h * at + NOPE : (h + 1) * at].astype(jnp.bfloat16)
            q_cols = pl.ds(pl.multiple_of(p * PAIR_Q + h * 128, 128), 256)
            for b in range(length // step):
                rows = slice(b * step, (b + 1) * step)
                end = (b + 1) * step
                scores = (
                    lax.dot_general(
                        queries[rows, q_cols],
                        keys[:end],
                        (((1,), (1,)), ((), ())),
                        preferred_element_type=jnp.float32,
                    )
                    * scale
                )
                last = jnp.where(diagonal, scores[:, b * step :], -1e30)
                scores = jnp.concatenate([scores[:, : b * step], last], axis=1) if b else last
                weights = jnp.exp(scores - jnp.max(scores, axis=1, keepdims=True))
                probs = (weights * (1.0 / jnp.sum(weights, axis=1, keepdims=True))).astype(
                    jnp.bfloat16
                )
                out = jnp.dot(probs, values[:end], preferred_element_type=jnp.float32)
                outs[rows, pl.ds(pl.multiple_of(p * PAIR_V + h * VDIM, 128), VDIM)] = out.astype(
                    jnp.bfloat16
                )

        @pl.when(p == 0)
        def _():
            pl.semaphore_wait(barrier, n_local - 1)

        for d in range(1, n_local):
            tell(p, d).start()
        own(p).start()
        return carry

    lax.fori_loop(0, pairs, pair, 0)

    rows = results[...].astype(jnp.float32).reshape(-1, results.shape[2]).astype(jnp.bfloat16)
    sums = jnp.dot(combine[0], rows, preferred_element_type=jnp.float32)
    for i in range(1, combine.shape[0]):
        sums += jnp.dot(combine[i], rows, preferred_element_type=jnp.float32)
    routed[...] = sums.astype(jnp.bfloat16)

    def settle(p, carry):
        for d in range(1, n_local):
            tell(p, d).wait()
        own(p).wait()
        return carry

    lax.fori_loop(0, pairs, settle, 0)


def shards(
    n_node,
    n_local,
    hidden,
    latent_weight,
    latent_gain,
    queries,
    kv_weight,
    expert_ids,
    route_weights,
    gate_proj,
    up_proj,
    down_proj,
):
    tokens, width = hidden.shape
    devices = n_node * n_local
    chips = devices // 2
    nz = 4 if n_node % 4 == 0 else n_node
    ny = n_node // nz
    bf16, f32 = jnp.bfloat16, jnp.float32

    present = jnp.arange(chips, dtype=jnp.int32) * (EXPERTS // chips)
    named = expert_ids[:, :, None] == present[None, None, :]
    member = jnp.any(named, axis=1)
    weight = jnp.sum(jnp.where(named, route_weights[:, :, None], 0.0), axis=1)
    at = jnp.arange(tokens, dtype=jnp.int32)
    earlier = (at[None, :] < at[:, None]).astype(bf16)
    slot = jnp.dot(earlier, member.astype(bf16), preferred_element_type=f32)
    slots = jnp.arange(CAP, dtype=jnp.int32).astype(f32)
    chosen = member[:, :, None] & (slot[:, :, None] == slots)
    pick = chosen.reshape(tokens, chips * CAP).astype(bf16).T
    dense = jnp.where(chosen, weight[:, :, None], 0.0).reshape(tokens, chips * CAP)
    high = lax.reduce_precision(dense, 8, 7)
    middle = lax.reduce_precision(dense - high, 8, 7)
    low = dense - high - middle
    combine = jnp.stack([high.astype(bf16), middle.astype(bf16), low.astype(bf16)])

    position = lax.axis_index("local") * tokens + at
    freqs = 10000.0 ** (-2.0 * jnp.arange(ROPE // 2, dtype=f32) / ROPE)
    angles = position.astype(f32)[:, None] * freqs[None, :]
    cosine, sine = jnp.cos(angles), jnp.sin(angles)
    cosine = jnp.concatenate([cosine, cosine], axis=1)
    sine = jnp.concatenate([-sine, sine], axis=1)

    half = latent_weight.shape[0] // 2
    total = latent_weight.shape[1]
    q_cols = queries.shape[1] // n_local
    vmem, hbm = pl.BlockSpec(memory_space=pltpu.VMEM), pl.BlockSpec(memory_space=pl.ANY)
    dma = pltpu.SemaphoreType.DMA
    chain = max(nz - 1, 1)
    gather = [dma((chain,))] * 4 + [dma((nz, max(ny - 1, 1)))] * 2
    others = max(n_local - 1, 1)
    width_e = gate_proj.shape[2]
    scratch = [
        pltpu.VMEM((n_node, 2, half, total), bf16),
        pltpu.VMEM((width, width_e), bf16),
        pltpu.VMEM((width, width_e), bf16),
        pltpu.VMEM((width_e, width), bf16),
        pltpu.VMEM((chips, CAP, width), bf16),
        pltpu.VMEM((2, chips, CAP, width), bf16),
        pltpu.VMEM((2, chips, CAP, width), bf16),
        pltpu.VMEM((chips, CAP, width), bf16),
        pltpu.VMEM((tokens, total), bf16),
        dma((9,)),
        *gather,
        *gather,
        dma((n_node,)),
        dma((n_node,)),
        *[dma((others,))] * 4,
        *[dma((chips - 1,))] * 4,
        dma((2,)),
        dma((2,)),
    ]

    def body(*refs):
        refs = list(refs)
        lat_sems, kv_sems = refs[25:31], refs[31:37]
        first_kernel(n_node, n_local, nz, *refs[:25], lat_sems, kv_sems, *refs[37:])

    sequence, head_queries, portion, results = pl.pallas_call(
        body,
        out_shape=(
            jax.ShapeDtypeStruct((n_local, tokens, total), bf16),
            jax.ShapeDtypeStruct((n_local, tokens, q_cols), bf16),
            jax.ShapeDtypeStruct((n_node, *kv_weight.shape), bf16),
            jax.ShapeDtypeStruct((chips, CAP, width), bf16),
        ),
        in_specs=[vmem] * 5 + [hbm] * 6,
        out_specs=(hbm,) * 4,
        scratch_shapes=scratch,
        compiler_params=pltpu.CompilerParams(
            collective_id=0, has_side_effects=True, vmem_limit_bytes=VMEM_LIMIT
        ),
        name="exchange",
    )(
        hidden,
        pick,
        latent_gain.reshape(1, -1),
        cosine,
        sine,
        latent_weight,
        queries,
        kv_weight,
        gate_proj,
        up_proj,
        down_proj,
    )

    length = n_local * tokens
    kv_cols = kv_weight.shape[1]
    pairs = kv_cols // PAIR_KV
    attention, routed = pl.pallas_call(
        functools.partial(second_kernel, n_node, n_local),
        out_shape=(
            jax.ShapeDtypeStruct((tokens, n_local * kv_cols // 2), bf16),
            jax.ShapeDtypeStruct((tokens, width), bf16),
        ),
        in_specs=[vmem] * 5,
        out_specs=(hbm, vmem),
        scratch_shapes=[
            pltpu.VMEM((length, kv_cols // 2), bf16),
            dma((pairs, others)),
            dma((pairs, others)),
            dma((pairs,)),
        ],
        compiler_params=pltpu.CompilerParams(
            collective_id=1, has_side_effects=True, vmem_limit_bytes=VMEM_LIMIT
        ),
        name="attend",
    )(
        sequence.reshape(length, total),
        head_queries.reshape(length, q_cols),
        portion.reshape(-1, kv_cols),
        results,
        combine,
    )
    return (attention, routed)


def solution(mesh):
    placed = (
        P(("node", "local"), None),
        P("node", None),
        P(),
        P(("node", "local"), None),
        P("node", "local"),
        P(("node", "local"), None),
        P(("node", "local"), None),
        P(("node", "local"), None, None),
        P(("node", "local"), None, None),
        P(("node", "local"), None, None),
    )
    return jax.shard_map(
        functools.partial(shards, mesh.shape["node"], mesh.shape["local"]),
        mesh=mesh,
        in_specs=placed,
        out_specs=(P(("node", "local"), None), P(("node", "local"), None)),
        check_vma=False,
    )
```

```python
import functools
import math
import types

import jax
import jax.numpy as jnp
import numpy as np
from jax import lax
from jax.experimental import pallas as pl
from jax.experimental.pallas import tpu as pltpu
from jax.sharding import PartitionSpec as P

NOPE = 128
ROPE = 64
VDIM = 128
LAT = 512
EXPERTS = 256
CAP = 8
PAIR_Q = 2 * (NOPE + ROPE)
PAIR_KV = 2 * (NOPE + VDIM)
PAIR_V = 2 * VDIM
MESH = pl.DeviceIdType.MESH
VMEM_LIMIT = 56 * 2**20


def remote(src, dst, send_sem, recv_sem, device):
    return pltpu.make_async_remote_copy(
        src_ref=src,
        dst_ref=dst,
        send_sem=send_sem,
        recv_sem=recv_sem,
        device_id=device,
        device_id_type=MESH,
    )


def greet(devices, n_local, me):
    barrier = pltpu.get_barrier_semaphore()

    def signal(d, carry):
        other = lax.rem(me + d, devices)
        pl.semaphore_signal(
            barrier,
            inc=1,
            device_id=(lax.div(other, n_local), lax.rem(other, n_local)),
            device_id_type=MESH,
        )
        return carry

    lax.fori_loop(1, devices, signal, 0)
    pl.semaphore_wait(barrier, devices - 1)


class Gather:
    def __init__(self, own, slot, nz, ny, node, local, sems):
        self.own, self.slot, self.nz, self.ny = own, slot, nz, ny
        self.z, self.y, self.local = lax.div(node, ny), lax.rem(node, ny), local
        self.up_s, self.up_r, self.dn_s, self.dn_r, self.y_s, self.y_r = sems

    def up(self, h, src):
        z = jnp.maximum(self.z - h, 0)
        dst = self.slot(z * self.ny + self.y)
        to = jnp.minimum(self.z + 1, self.nz - 1)
        return remote(
            dst if src is None else src, dst, self.up_s.at[h], self.up_r.at[h], (to * self.ny + self.y, self.local)
        )

    def down(self, h, src):
        z = jnp.minimum(self.z + h, self.nz - 1)
        dst = self.slot(z * self.ny + self.y)
        to = jnp.maximum(self.z - 1, 0)
        return remote(
            dst if src is None else src, dst, self.dn_s.at[h], self.dn_r.at[h], (to * self.ny + self.y, self.local)
        )

    def across(self, z, dy, src):
        dst = self.slot(z * self.ny + self.y)
        to = self.z * self.ny + lax.rem(self.y + dy, self.ny)
        return remote(
            dst if src is None else src, dst, self.y_s.at[z, dy - 1], self.y_r.at[z, dy - 1], (to, self.local)
        )

    def begin(self):
        @pl.when(self.z < self.nz - 1)
        def _():
            self.up(0, self.own).start()

        @pl.when(self.z > 0)
        def _():
            self.down(0, self.own).start()

        for dy in range(1, self.ny):
            self.across(self.z, dy, self.own).start()

    def hop(self, h, landed=None):
        @pl.when(self.z - h >= 0)
        def _():
            self.up(h - 1, None).wait_recv()
            if h < self.nz - 1:

                @pl.when(self.z < self.nz - 1)
                def _():
                    self.up(h, None).start()

            for dy in range(1, self.ny):
                self.across(self.z - h, dy, None).start()
            if landed:
                landed((self.z - h) * self.ny + self.y)

        @pl.when(self.z + h < self.nz)
        def _():
            self.down(h - 1, None).wait_recv()
            if h < self.nz - 1:

                @pl.when(self.z > 0)
                def _():
                    self.down(h, None).start()

            for dy in range(1, self.ny):
                self.across(self.z + h, dy, None).start()
            if landed:
                landed((self.z + h) * self.ny + self.y)

    def columns(self, landed=None):
        for z in range(self.nz):
            for dy in range(1, self.ny):
                self.across(z, dy, None).wait_recv()
                if landed:
                    landed(z * self.ny + lax.rem(self.y - dy + self.ny, self.ny))

    def finish(self):
        for h in range(self.nz - 1):

            @pl.when((self.z < self.nz - 1) & (self.z - h >= 0))
            def _():
                self.up(h, None).wait_send()

            @pl.when((self.z > 0) & (self.z + h < self.nz))
            def _():
                self.down(h, None).wait_send()

        for z in range(self.nz):
            for dy in range(1, self.ny):
                self.across(z, dy, None).wait_send()


def present_routes(ids, gates, tokens, chips, stride):
    shape = (tokens, chips * CAP)
    lane = lax.broadcasted_iota(jnp.int32, shape, 1)
    expert = lax.div(lane, CAP) * stride
    count = jnp.zeros(shape, jnp.float32)
    weight = jnp.zeros(shape, jnp.float32)
    for k in range(ids.shape[1]):
        hit = ids[:, k : k + 1] == expert
        count += jnp.where(hit, 1.0, 0.0)
        weight += jnp.where(hit, gates[:, k : k + 1], 0.0)
    square = (tokens, tokens)
    earlier = lax.broadcasted_iota(jnp.int32, square, 1) < lax.broadcasted_iota(
        jnp.int32, square, 0
    )
    slot = jnp.dot(
        jnp.where(earlier, 1.0, 0.0).astype(jnp.bfloat16),
        count.astype(jnp.bfloat16),
        preferred_element_type=jnp.float32,
    )
    chosen = jnp.where(slot == lax.rem(lane, CAP).astype(jnp.float32), count, 0.0)
    return chosen, chosen * weight


def block_kernel(n_node, n_local, nz, stride, r):
    node, local = lax.axis_index("node"), lax.axis_index("local")
    devices, ny = n_node * n_local, n_node // nz
    chips = devices // 2
    me = node * n_local + local
    chip, core = lax.div(me, 2), lax.rem(me, 2)
    sibling = (node, local + 1 - 2 * core)
    half = r.lat.shape[2]
    tokens = r.hidden.shape[0]
    q_cols = r.q.shape[2]
    length = n_local * tokens
    pairs = r.kv.shape[2] // PAIR_KV
    wide = r.kv.shape[2] // 2
    front = pairs // 2

    own_q = pl.ds(pl.multiple_of(local * q_cols, 128), q_cols)
    weights_in = [
        pltpu.make_async_copy(r.gate_w.at[0], r.gates, r.local_sem.at[0]),
        pltpu.make_async_copy(r.up_w.at[0], r.ups, r.local_sem.at[1]),
        pltpu.make_async_copy(r.down_w.at[0], r.downs, r.local_sem.at[2]),
    ]
    kv_in = pltpu.make_async_copy(r.kv_w, r.kv.at[node], r.local_sem.at[3])
    q_in = pltpu.make_async_copy(r.queries.at[:, own_q], r.q.at[local], r.local_sem.at[4])
    lat_in = [
        pltpu.make_async_copy(
            r.latent_w.at[pl.ds(i * half, half)], r.lat.at[node, i], r.local_sem.at[5 + i]
        )
        for i in range(2)
    ]

    greet(devices, n_local, me)

    def device_of(c):
        dev = c * 2 + core
        return (lax.div(dev, n_local), lax.rem(dev, n_local))

    def go(d):
        to = lax.rem(chip + d, chips)
        return remote(
            r.leaving.at[to],
            r.arrived.at[core, chip],
            r.go_s.at[d - 1],
            r.go_r.at[d - 1],
            device_of(to),
        )

    def back(d):
        to = lax.rem(chip + d, chips)
        return remote(
            r.part.at[core, to],
            r.results.at[chip],
            r.back_s.at[d - 1],
            r.back_r.at[d - 1],
            device_of(to),
        )

    def each(first, last, act):
        def step(d, carry):
            act(d)
            return carry

        lax.fori_loop(first, last, step, 0)

    def ask(d):
        to = lax.rem(local + d, n_local)
        cols = pl.ds(pl.multiple_of(to * q_cols, 128), q_cols)
        return remote(
            r.queries.at[:, cols], r.q.at[local], r.q_s.at[d - 1], r.q_r.at[d - 1], (node, to)
        )

    lat_gather = Gather(
        r.latent_w.at[pl.ds(pl.multiple_of(core * half, 16), half)],
        lambda n: r.lat.at[n, core],
        nz,
        ny,
        node,
        local,
        r.lat_sems,
    )
    near = pl.ds(0, front * PAIR_KV)
    far = pl.ds(front * PAIR_KV, (pairs - front) * PAIR_KV)
    kv_near = Gather(
        r.kv_w.at[:, near], lambda n: r.kv.at[n, :, near], nz, ny, node, local, r.near_sems
    )
    kv_far = Gather(
        r.kv_w.at[:, far], lambda n: r.kv.at[n, :, far], nz, ny, node, local, r.far_sems
    )

    def share(n):
        return remote(
            r.lat.at[n, core], r.lat.at[n, core], r.core_s.at[n], r.core_r.at[n], sibling
        )

    def landed(n):
        share(n).start()

    lat_gather.begin()
    kv_near.begin()
    for d in range(1, n_local):
        ask(d).start()
    for copy in (*lat_in, kv_in, q_in, *weights_in):
        copy.start()

    chosen, dense = present_routes(r.ids, r.route_w, tokens, chips, stride)
    r.dense[...] = dense
    rows = lax.dot_general(
        chosen.astype(jnp.bfloat16),
        r.hidden[...],
        (((0,), (0,)), ((), ())),
        preferred_element_type=jnp.float32,
    )
    r.leaving[...] = rows.reshape(r.leaving.shape).astype(jnp.bfloat16)
    r.arrived[core, chip] = r.leaving[chip]

    for h in range(1, nz):
        lat_gather.hop(h, landed)
        kv_near.hop(h)
        if h == max(nz - 2, 1):
            each(1, chips, lambda d: go(d).start())
    kv_far.begin()

    lat_gather.columns(landed)

    def shared(n, carry):
        @pl.when(n != node)
        def _():
            remote(
                r.lat.at[n, 1 - core],
                r.lat.at[n, 1 - core],
                r.core_s.at[n],
                r.core_r.at[n],
                sibling,
            ).wait_recv()

        return carry

    lax.fori_loop(0, n_node, shared, 0)
    for copy in lat_in:
        copy.wait()
    weight = r.lat[...].reshape(n_node * 2 * half, r.lat.shape[3])
    latent = jnp.dot(r.hidden[...], weight, preferred_element_type=jnp.float32)
    u = latent[:, :LAT]
    norm = lax.rsqrt(jnp.mean(u * u, axis=1, keepdims=True) + 1e-06)
    r.mine[:, :LAT] = (u * norm * r.gain[...]).astype(jnp.bfloat16)
    a = latent[:, LAT:]
    swapped = jnp.concatenate([a[:, ROPE // 2 :], a[:, : ROPE // 2]], axis=1)
    turn = r.turns[pl.ds(pl.multiple_of(local * tokens, 16), tokens)]
    r.mine[:, LAT:] = (a * turn[:, :ROPE] + swapped * turn[:, ROPE:]).astype(jnp.bfloat16)

    def tell(d):
        to = lax.rem(local + d, n_local)
        return remote(
            r.mine, r.seq.at[local], r.seq_s.at[d - 1], r.seq_r.at[d - 1], (node, to)
        )

    for d in range(1, n_local):
        tell(d).start()
    r.seq[local] = r.mine[...]

    if nz > 1:
        kv_far.hop(1)
    kv_near.columns()
    kv_in.wait()
    q_in.wait()
    for d in range(1, n_local):
        ask(d).wait()
        tell(d).wait()

    scale = math.log2(math.e) / math.sqrt(NOPE + ROPE)
    step = 256
    diagonal = lax.broadcasted_iota(jnp.int32, (step, step), 1) <= lax.broadcasted_iota(
        jnp.int32, (step, step), 0
    )

    def place(p):
        return pl.ds(pl.multiple_of(local * wide + p * PAIR_V, 128), PAIR_V)

    def out_cols(p):
        return pl.ds(pl.multiple_of(p * PAIR_V, 128), PAIR_V)

    def reply(p, d):
        to = lax.rem(local + d, n_local)
        rows = pl.ds(pl.multiple_of(to * tokens, 16), tokens)
        return remote(
            r.outs.at[rows, out_cols(p)],
            r.attention.at[:, place(p)],
            r.out_s.at[p, d - 1],
            r.out_r.at[p, d - 1],
            (node, to),
        )

    def keep(p):
        rows = pl.ds(pl.multiple_of(local * tokens, 16), tokens)
        return pltpu.make_async_copy(
            r.outs.at[rows, out_cols(p)], r.attention.at[:, place(p)], r.keep.at[p]
        )

    def pair(p, carry):
        cols = pl.ds(pl.multiple_of(p * PAIR_KV, 128), PAIR_KV)
        compressed = r.seq[:, :, :LAT].reshape(length, LAT)
        rope = r.seq[:, :, LAT:].reshape(length, ROPE).astype(jnp.float32)
        zeros = jnp.zeros((length, 128 - ROPE), jnp.float32)
        up = r.kv[:, :, cols].reshape(LAT, PAIR_KV)
        keyval = jnp.dot(compressed, up, preferred_element_type=jnp.float32)
        first = jnp.concatenate([keyval[:, :NOPE], rope, zeros], axis=1).astype(jnp.bfloat16)
        at = NOPE + VDIM
        second = jnp.concatenate([zeros, keyval[:, at : at + NOPE], rope], axis=1).astype(
            jnp.bfloat16
        )
        for h, keys in enumerate((first, second)):
            values = keyval[:, h * at + NOPE : (h + 1) * at].astype(jnp.bfloat16)
            window = pl.ds(pl.multiple_of(p * PAIR_Q + h * 128, 128), 256)
            asked = r.q[:, :, window].reshape(length, 256)
            for b in range(length // step):
                end = (b + 1) * step
                scores = lax.dot_general(
                    asked[b * step : end],
                    keys[:end],
                    (((1,), (1,)), ((), ())),
                    preferred_element_type=jnp.float32,
                )
                last = jnp.where(diagonal, scores[:, b * step :], -1e30)
                scores = jnp.concatenate([scores[:, : b * step], last], axis=1) if b else last
                weights = jnp.exp2((scores - jnp.max(scores, axis=1, keepdims=True)) * scale)
                probs = (weights * (1.0 / jnp.sum(weights, axis=1, keepdims=True))).astype(
                    jnp.bfloat16
                )
                out = jnp.dot(probs, values[:end], preferred_element_type=jnp.float32)
                spot = pl.ds(pl.multiple_of(p * PAIR_V + h * VDIM, 128), VDIM)
                r.outs[b * step : end, spot] = out.astype(jnp.bfloat16)
        for d in range(1, n_local):
            reply(p, d).start()
        keep(p).start()
        return carry

    early = max(front // 2, 1)
    lax.fori_loop(0, early, pair, 0)
    if nz > 2:
        kv_far.hop(2)
    lax.fori_loop(early, front, pair, 0)
    for h in range(3, nz):
        kv_far.hop(h)

    each(1, chips, lambda d: go(d).wait_recv())
    swap = remote(
        r.arrived.at[core], r.arrived.at[core], r.sib_s.at[0], r.sib_r.at[0], sibling
    )
    swap.start()
    for copy in weights_in:
        copy.wait()
    swap.wait()

    batch = min(32, chips)
    per = chips // batch

    def expert(i, carry):
        c, p = lax.div(i, per), lax.rem(i, per)
        at = pl.ds(p * batch, batch)
        x = r.arrived[c, at].astype(jnp.float32).reshape(batch * CAP, -1).astype(jnp.bfloat16)
        gate = jnp.dot(x, r.gates[...], preferred_element_type=jnp.float32)
        upper = jnp.dot(x, r.ups[...], preferred_element_type=jnp.float32)
        inner = (gate / (1.0 + jnp.exp(-gate)) * upper).astype(jnp.bfloat16)
        width = r.downs.shape[1] // 7
        for j in range(7):
            cols = slice(j * width, (j + 1) * width)
            y = jnp.dot(inner, r.downs[:, cols], preferred_element_type=jnp.float32)
            r.part[c, at, :, cols] = y.reshape(batch, CAP, width).astype(jnp.bfloat16)
        return carry

    lax.fori_loop(0, 2 * per, expert, 0)
    give = remote(r.part.at[1 - core], r.sibpart, r.sib_s.at[1], r.sib_r.at[1], sibling)
    give.start()
    kv_far.columns()
    give.wait()

    def total(p, carry):
        both = r.part[core, p].astype(jnp.float32) + r.sibpart[p].astype(jnp.float32)
        r.part[core, p] = both.astype(jnp.bfloat16)
        return carry

    lax.fori_loop(0, chips, total, 0)
    each(1, chips, lambda d: back(d).start())
    r.results[chip] = r.part[core, chip]

    lax.fori_loop(front, pairs, pair, 0)

    each(1, chips, lambda d: back(d).wait())
    dense = r.dense[...]
    high = dense.astype(jnp.bfloat16)
    rest = dense - high.astype(jnp.float32)
    middle = rest.astype(jnp.bfloat16)
    low = (rest - middle.astype(jnp.float32)).astype(jnp.bfloat16)
    width = r.results.shape[2] // 7
    for j in range(7):
        cols = slice(j * width, (j + 1) * width)
        rows = (
            r.results[:, :, cols]
            .astype(jnp.float32)
            .reshape(chips * CAP, width)
            .astype(jnp.bfloat16)
        )
        sums = jnp.dot(high, rows, preferred_element_type=jnp.float32)
        sums += jnp.dot(middle, rows, preferred_element_type=jnp.float32)
        sums += jnp.dot(low, rows, preferred_element_type=jnp.float32)
        r.routed[:, cols] = sums.astype(jnp.bfloat16)

    each(1, chips, lambda d: go(d).wait_send())
    lat_gather.finish()
    kv_near.finish()
    kv_far.finish()

    def shared_sent(n, carry):
        @pl.when(n != node)
        def _():
            share(n).wait_send()

        return carry

    lax.fori_loop(0, n_node, shared_sent, 0)

    def settle(p, carry):
        for d in range(1, n_local):
            reply(p, d).wait()
        keep(p).wait()
        return carry

    lax.fori_loop(0, pairs, settle, 0)


def shards(
    n_node,
    n_local,
    hidden,
    latent_weight,
    latent_gain,
    queries,
    kv_weight,
    expert_ids,
    route_weights,
    gate_proj,
    up_proj,
    down_proj,
):
    tokens, width = hidden.shape
    chips = n_node * n_local // 2
    nz = 4 if n_node % 4 == 0 else n_node
    ny = n_node // nz
    bf16, f32 = jnp.bfloat16, jnp.float32
    length = n_local * tokens

    freqs = 10000.0 ** (-2.0 * np.arange(ROPE // 2) / ROPE)
    angles = np.arange(length)[:, None] * freqs[None, :]
    cosine, sine = np.cos(angles), np.sin(angles)
    turns = jnp.asarray(np.concatenate([cosine, cosine, -sine, sine], axis=1), f32)

    half = latent_weight.shape[0] // 2
    total = latent_weight.shape[1]
    kv_rows, kv_cols = kv_weight.shape
    q_cols = queries.shape[1] // n_local
    pairs = kv_cols // PAIR_KV
    vmem, hbm = pl.BlockSpec(memory_space=pltpu.VMEM), pl.BlockSpec(memory_space=pl.ANY)
    dma = pltpu.SemaphoreType.DMA
    chain = max(nz - 1, 1)
    gather = [dma((chain,))] * 4 + [dma((nz, max(ny - 1, 1)))] * 2
    others = max(n_local - 1, 1)
    width_e = gate_proj.shape[2]
    operands = dict(
        hidden=hidden,
        ids=expert_ids,
        route_w=route_weights,
        gain=latent_gain.reshape(1, -1),
        turns=turns,
        latent_w=latent_weight,
        queries=queries,
        kv_w=kv_weight,
        gate_w=gate_proj,
        up_w=up_proj,
        down_w=down_proj,
    )
    scratch = dict(
        lat=pltpu.VMEM((n_node, 2, half, total), bf16),
        kv=pltpu.VMEM((n_node, kv_rows, kv_cols), bf16),
        q=pltpu.VMEM((n_local, tokens, q_cols), bf16),
        seq=pltpu.VMEM((n_local, tokens, total), bf16),
        outs=pltpu.VMEM((length, kv_cols // 2), bf16),
        gates=pltpu.VMEM((width, width_e), bf16),
        ups=pltpu.VMEM((width, width_e), bf16),
        downs=pltpu.VMEM((width_e, width), bf16),
        leaving=pltpu.VMEM((chips, CAP, width), bf16),
        arrived=pltpu.VMEM((2, chips, CAP, width), bf16),
        part=pltpu.VMEM((2, chips, CAP, width), bf16),
        sibpart=pltpu.VMEM((chips, CAP, width), bf16),
        results=pltpu.VMEM((chips, CAP, width), bf16),
        mine=pltpu.VMEM((tokens, total), bf16),
        dense=pltpu.VMEM((tokens, chips * CAP), f32),
        local_sem=dma((7,)),
        core_s=dma((n_node,)),
        core_r=dma((n_node,)),
        q_s=dma((others,)),
        q_r=dma((others,)),
        seq_s=dma((others,)),
        seq_r=dma((others,)),
        go_s=dma((chips - 1,)),
        go_r=dma((chips - 1,)),
        back_s=dma((chips - 1,)),
        back_r=dma((chips - 1,)),
        sib_s=dma((2,)),
        sib_r=dma((2,)),
        out_s=dma((pairs, others)),
        out_r=dma((pairs, others)),
        keep=dma((pairs,)),
    )
    names = [*operands, "attention", "routed", *scratch]

    def body(*refs):
        r = types.SimpleNamespace(**dict(zip(names, refs)))
        rest = refs[len(names) :]
        r.lat_sems, r.near_sems, r.far_sems = rest[:6], rest[6:12], rest[12:]
        block_kernel(n_node, n_local, nz, EXPERTS // chips, r)

    return pl.pallas_call(
        body,
        out_shape=(
            jax.ShapeDtypeStruct((tokens, n_local * kv_cols // 2), bf16),
            jax.ShapeDtypeStruct((tokens, width), bf16),
        ),
        in_specs=[vmem] * 5 + [hbm] * 6,
        out_specs=(hbm, vmem),
        scratch_shapes=[*scratch.values(), *gather * 3],
        compiler_params=pltpu.CompilerParams(
            collective_id=0, has_side_effects=True, vmem_limit_bytes=VMEM_LIMIT
        ),
        name="block",
    )(*operands.values())


def solution(mesh):
    placed = (
        P(("node", "local"), None),
        P("node", None),
        P(),
        P(("node", "local"), None),
        P("node", "local"),
        P(("node", "local"), None),
        P(("node", "local"), None),
        P(("node", "local"), None, None),
        P(("node", "local"), None, None),
        P(("node", "local"), None, None),
    )
    return jax.shard_map(
        functools.partial(shards, mesh.shape["node"], mesh.shape["local"]),
        mesh=mesh,
        in_specs=placed,
        out_specs=(P(("node", "local"), None), P(("node", "local"), None)),
        check_vma=False,
    )
```

```python
import functools
import math
import types

import jax
import jax.numpy as jnp
import numpy as np
from jax import lax
from jax.experimental import pallas as pl
from jax.experimental.pallas import tpu as pltpu
from jax.sharding import PartitionSpec as P

NOPE = 128
ROPE = 64
VDIM = 128
LAT = 512
EXPERTS = 256
CAP = 8
PAIR_Q = 2 * (NOPE + ROPE)
PAIR_KV = 2 * (NOPE + VDIM)
PAIR_V = 2 * VDIM
MESH = pl.DeviceIdType.MESH
VMEM_LIMIT = 56 * 2**20


def remote(src, dst, send_sem, recv_sem, device):
    return pltpu.make_async_remote_copy(
        src_ref=src,
        dst_ref=dst,
        send_sem=send_sem,
        recv_sem=recv_sem,
        device_id=device,
        device_id_type=MESH,
    )


def greet(devices, n_local, me):
    barrier = pltpu.get_barrier_semaphore()

    def signal(d, carry):
        other = lax.rem(me + d, devices)
        pl.semaphore_signal(
            barrier,
            inc=1,
            device_id=(lax.div(other, n_local), lax.rem(other, n_local)),
            device_id_type=MESH,
        )
        return carry

    lax.fori_loop(1, devices, signal, 0)
    pl.semaphore_wait(barrier, devices - 1)


class Gather:
    def __init__(self, own, slot, nz, ny, node, local, sems):
        self.own, self.slot, self.nz, self.ny = own, slot, nz, ny
        self.z, self.y, self.local = lax.div(node, ny), lax.rem(node, ny), local
        self.up_s, self.up_r, self.dn_s, self.dn_r, self.y_s, self.y_r = sems

    def up(self, h, src):
        z = jnp.maximum(self.z - h, 0)
        dst = self.slot(z * self.ny + self.y)
        to = jnp.minimum(self.z + 1, self.nz - 1)
        return remote(
            dst if src is None else src, dst, self.up_s.at[h], self.up_r.at[h], (to * self.ny + self.y, self.local)
        )

    def down(self, h, src):
        z = jnp.minimum(self.z + h, self.nz - 1)
        dst = self.slot(z * self.ny + self.y)
        to = jnp.maximum(self.z - 1, 0)
        return remote(
            dst if src is None else src, dst, self.dn_s.at[h], self.dn_r.at[h], (to * self.ny + self.y, self.local)
        )

    def across(self, z, dy, src):
        dst = self.slot(z * self.ny + self.y)
        to = self.z * self.ny + lax.rem(self.y + dy, self.ny)
        return remote(
            dst if src is None else src, dst, self.y_s.at[z, dy - 1], self.y_r.at[z, dy - 1], (to, self.local)
        )

    def begin(self):
        @pl.when(self.z < self.nz - 1)
        def _():
            self.up(0, self.own).start()

        @pl.when(self.z > 0)
        def _():
            self.down(0, self.own).start()

        for dy in range(1, self.ny):
            self.across(self.z, dy, self.own).start()

    def hop(self, h, landed=None):
        @pl.when(self.z - h >= 0)
        def _():
            self.up(h - 1, None).wait_recv()
            if h < self.nz - 1:

                @pl.when(self.z < self.nz - 1)
                def _():
                    self.up(h, None).start()

            for dy in range(1, self.ny):
                self.across(self.z - h, dy, None).start()
            if landed:
                landed((self.z - h) * self.ny + self.y)

        @pl.when(self.z + h < self.nz)
        def _():
            self.down(h - 1, None).wait_recv()
            if h < self.nz - 1:

                @pl.when(self.z > 0)
                def _():
                    self.down(h, None).start()

            for dy in range(1, self.ny):
                self.across(self.z + h, dy, None).start()
            if landed:
                landed((self.z + h) * self.ny + self.y)

    def columns(self, landed=None):
        for z in range(self.nz):
            for dy in range(1, self.ny):
                self.across(z, dy, None).wait_recv()
                if landed:
                    landed(z * self.ny + lax.rem(self.y - dy + self.ny, self.ny))

    def finish(self):
        for h in range(self.nz - 1):

            @pl.when((self.z < self.nz - 1) & (self.z - h >= 0))
            def _():
                self.up(h, None).wait_send()

            @pl.when((self.z > 0) & (self.z + h < self.nz))
            def _():
                self.down(h, None).wait_send()

        for z in range(self.nz):
            for dy in range(1, self.ny):
                self.across(z, dy, None).wait_send()


def present_routes(ids, gates, tokens, chips, stride):
    shape = (chips * CAP, tokens)
    row = lax.broadcasted_iota(jnp.int32, shape, 0)
    expert = lax.div(row, CAP) * stride
    count = jnp.zeros(shape, jnp.float32)
    weight = jnp.zeros(shape, jnp.float32)
    for k in range(ids.shape[0]):
        hit = ids[k : k + 1, :] == expert
        count += jnp.where(hit, 1.0, 0.0)
        weight += jnp.where(hit, gates[k : k + 1, :], 0.0)
    square = (tokens, tokens)
    earlier = lax.broadcasted_iota(jnp.int32, square, 0) < lax.broadcasted_iota(
        jnp.int32, square, 1
    )
    slot = jnp.dot(
        count.astype(jnp.bfloat16),
        jnp.where(earlier, 1.0, 0.0).astype(jnp.bfloat16),
        preferred_element_type=jnp.float32,
    )
    chosen = jnp.where(slot == lax.rem(row, CAP).astype(jnp.float32), count, 0.0)
    return chosen, chosen * weight


def block_kernel(n_node, n_local, nz, stride, r):
    node, local = lax.axis_index("node"), lax.axis_index("local")
    devices, ny = n_node * n_local, n_node // nz
    chips = devices // 2
    me = node * n_local + local
    chip, core = lax.div(me, 2), lax.rem(me, 2)
    sibling = (node, local + 1 - 2 * core)
    half = r.lat.shape[2]
    tokens = r.hidden.shape[0]
    q_cols = r.q.shape[2]
    length = n_local * tokens
    pairs = r.kv.shape[2] // PAIR_KV
    wide = r.kv.shape[2] // 2
    front = pairs // 2

    own_q = pl.ds(pl.multiple_of(local * q_cols, 128), q_cols)
    weights_in = [
        pltpu.make_async_copy(r.gate_w.at[0], r.gates, r.local_sem.at[0]),
        pltpu.make_async_copy(r.up_w.at[0], r.ups, r.local_sem.at[1]),
        pltpu.make_async_copy(r.down_w.at[0], r.downs, r.local_sem.at[2]),
    ]
    kv_in = pltpu.make_async_copy(r.kv_w, r.kv.at[node], r.local_sem.at[3])
    q_in = pltpu.make_async_copy(r.queries.at[:, own_q], r.q.at[local], r.local_sem.at[4])
    lat_in = [
        pltpu.make_async_copy(
            r.latent_w.at[pl.ds(i * half, half)], r.lat.at[node, i], r.local_sem.at[5 + i]
        )
        for i in range(2)
    ]

    for copy in (*lat_in, kv_in, q_in, *weights_in):
        copy.start()

    chosen, dense = present_routes(r.ids, r.route_w, tokens, chips, stride)
    r.dense[...] = dense
    rows = jnp.dot(
        chosen.astype(jnp.bfloat16), r.hidden[...], preferred_element_type=jnp.float32
    )
    r.leaving[...] = rows.reshape(r.leaving.shape).astype(jnp.bfloat16)
    r.arrived[core, chip] = r.leaving[chip]

    greet(devices, n_local, me)

    def device_of(c):
        dev = c * 2 + core
        return (lax.div(dev, n_local), lax.rem(dev, n_local))

    def go(d):
        to = lax.rem(chip + d, chips)
        return remote(
            r.leaving.at[to],
            r.arrived.at[core, chip],
            r.go_s.at[d - 1],
            r.go_r.at[d - 1],
            device_of(to),
        )

    def back(d):
        to = lax.rem(chip + d, chips)
        return remote(
            r.part.at[core, to],
            r.results.at[chip],
            r.back_s.at[d - 1],
            r.back_r.at[d - 1],
            device_of(to),
        )

    def each(first, last, act):
        def step(d, carry):
            act(d)
            return carry

        lax.fori_loop(first, last, step, 0)

    def ask(d):
        to = lax.rem(local + d, n_local)
        cols = pl.ds(pl.multiple_of(to * q_cols, 128), q_cols)
        return remote(
            r.queries.at[:, cols], r.q.at[local], r.q_s.at[d - 1], r.q_r.at[d - 1], (node, to)
        )

    lat_gather = Gather(
        r.latent_w.at[pl.ds(pl.multiple_of(core * half, 16), half)],
        lambda n: r.lat.at[n, core],
        nz,
        ny,
        node,
        local,
        r.lat_sems,
    )
    near = pl.ds(0, front * PAIR_KV)
    far = pl.ds(front * PAIR_KV, (pairs - front) * PAIR_KV)
    kv_near = Gather(
        r.kv_w.at[:, near], lambda n: r.kv.at[n, :, near], nz, ny, node, local, r.near_sems
    )
    kv_far = Gather(
        r.kv_w.at[:, far], lambda n: r.kv.at[n, :, far], nz, ny, node, local, r.far_sems
    )

    def share(n):
        return remote(
            r.lat.at[n, core], r.lat.at[n, core], r.core_s.at[n], r.core_r.at[n], sibling
        )

    def landed(n):
        share(n).start()

    lat_gather.begin()
    each(1, chips, lambda d: go(d).start())
    kv_near.begin()
    for d in range(1, n_local):
        ask(d).start()

    for h in range(1, nz):
        lat_gather.hop(h, landed)
        kv_near.hop(h)
    kv_far.begin()

    lat_gather.columns(landed)
    each(1, chips, lambda d: go(d).wait_recv())
    swap = remote(
        r.arrived.at[core], r.arrived.at[core], r.sib_s.at[0], r.sib_r.at[0], sibling
    )
    swap.start()

    def shared(n, carry):
        @pl.when(n != node)
        def _():
            remote(
                r.lat.at[n, 1 - core],
                r.lat.at[n, 1 - core],
                r.core_s.at[n],
                r.core_r.at[n],
                sibling,
            ).wait_recv()

        return carry

    lax.fori_loop(0, n_node, shared, 0)
    for copy in lat_in:
        copy.wait()
    weight = r.lat[...].reshape(n_node * 2 * half, r.lat.shape[3])
    latent = jnp.dot(r.hidden[...], weight, preferred_element_type=jnp.float32)
    u = latent[:, :LAT]
    norm = lax.rsqrt(jnp.mean(u * u, axis=1, keepdims=True) + 1e-06)
    r.mine[:, :LAT] = (u * norm * r.gain[...]).astype(jnp.bfloat16)
    a = latent[:, LAT:]
    swapped = jnp.concatenate([a[:, ROPE // 2 :], a[:, : ROPE // 2]], axis=1)
    turn = r.turns[pl.ds(pl.multiple_of(local * tokens, 16), tokens)]
    r.mine[:, LAT:] = (a * turn[:, :ROPE] + swapped * turn[:, ROPE:]).astype(jnp.bfloat16)

    def tell(d):
        to = lax.rem(local + d, n_local)
        return remote(
            r.mine, r.seq.at[local], r.seq_s.at[d - 1], r.seq_r.at[d - 1], (node, to)
        )

    for d in range(1, n_local):
        tell(d).start()
    r.seq[local] = r.mine[...]

    if nz > 1:
        kv_far.hop(1)

    for copy in weights_in:
        copy.wait()
    swap.wait()

    batch = min(32, chips)
    per = chips // batch

    def expert(i, carry):
        c, p = lax.div(i, per), lax.rem(i, per)
        at = pl.ds(p * batch, batch)
        x = r.arrived[c, at].astype(jnp.float32).reshape(batch * CAP, -1).astype(jnp.bfloat16)
        gate = jnp.dot(x, r.gates[...], preferred_element_type=jnp.float32)
        upper = jnp.dot(x, r.ups[...], preferred_element_type=jnp.float32)
        inner = (gate / (1.0 + jnp.exp(-gate)) * upper).astype(jnp.bfloat16)
        width = r.downs.shape[1] // 7
        for j in range(7):
            cols = slice(j * width, (j + 1) * width)
            y = jnp.dot(inner, r.downs[:, cols], preferred_element_type=jnp.float32)
            r.part[c, at, :, cols] = y.reshape(batch, CAP, width).astype(jnp.bfloat16)
        return carry

    lax.fori_loop(0, 2 * per, expert, 0)
    give = remote(r.part.at[1 - core], r.sibpart, r.sib_s.at[1], r.sib_r.at[1], sibling)
    give.start()
    if nz > 2:
        kv_far.hop(2)
    give.wait()

    def total(p, carry):
        both = r.part[core, p].astype(jnp.float32) + r.sibpart[p].astype(jnp.float32)
        r.part[core, p] = both.astype(jnp.bfloat16)
        return carry

    lax.fori_loop(0, chips, total, 0)
    each(1, chips, lambda d: back(d).start())
    kept = pltpu.make_async_copy(r.part.at[core, chip], r.results.at[chip], r.local_sem.at[7])
    kept.start()
    for h in range(3, nz):
        kv_far.hop(h)

    kv_near.columns()
    kv_in.wait()
    q_in.wait()
    for d in range(1, n_local):
        ask(d).wait()
        tell(d).wait()

    scale = math.log2(math.e) / math.sqrt(NOPE + ROPE)
    step = 256
    diagonal = lax.broadcasted_iota(jnp.int32, (step, step), 1) <= lax.broadcasted_iota(
        jnp.int32, (step, step), 0
    )

    def place(p):
        return pl.ds(pl.multiple_of(local * wide + p * PAIR_V, 128), PAIR_V)

    def out_cols(p):
        return pl.ds(pl.multiple_of(p * PAIR_V, 128), PAIR_V)

    def reply(p, d):
        to = lax.rem(local + d, n_local)
        rows = pl.ds(pl.multiple_of(to * tokens, 16), tokens)
        return remote(
            r.outs.at[rows, out_cols(p)],
            r.attention.at[:, place(p)],
            r.out_s.at[p, d - 1],
            r.out_r.at[p, d - 1],
            (node, to),
        )

    def keep(p):
        rows = pl.ds(pl.multiple_of(local * tokens, 16), tokens)
        return pltpu.make_async_copy(
            r.outs.at[rows, out_cols(p)], r.attention.at[:, place(p)], r.keep.at[p]
        )

    def pair(p, carry):
        cols = pl.ds(pl.multiple_of(p * PAIR_KV, 128), PAIR_KV)
        compressed = r.seq[:, :, :LAT].reshape(length, LAT)
        rope = r.seq[:, :, LAT:].reshape(length, ROPE).astype(jnp.float32)
        zeros = jnp.zeros((length, 128 - ROPE), jnp.float32)
        ones = jnp.ones((length, VDIM), jnp.bfloat16)
        up = r.kv[:, :, cols].reshape(LAT, PAIR_KV)
        keyval = jnp.dot(compressed, up, preferred_element_type=jnp.float32)
        first = jnp.concatenate([keyval[:, :NOPE], rope, zeros], axis=1).astype(jnp.bfloat16)
        at = NOPE + VDIM
        second = jnp.concatenate([zeros, keyval[:, at : at + NOPE], rope], axis=1).astype(
            jnp.bfloat16
        )
        for h, keys in enumerate((first, second)):
            values = jnp.concatenate(
                [keyval[:, h * at + NOPE : (h + 1) * at].astype(jnp.bfloat16), ones], axis=1
            )
            window = pl.ds(pl.multiple_of(p * PAIR_Q + h * 128, 128), 256)
            asked = r.q[:, :, window].reshape(length, 256)
            for b in range(length // step):
                end = (b + 1) * step
                scores = lax.dot_general(
                    asked[b * step : end],
                    keys[:end],
                    (((1,), (1,)), ((), ())),
                    preferred_element_type=jnp.float32,
                )
                last = jnp.where(diagonal, scores[:, b * step :], -1e30)
                scores = jnp.concatenate([scores[:, : b * step], last], axis=1) if b else last
                weights = jnp.exp2((scores - jnp.max(scores, axis=1, keepdims=True)) * scale)
                both = jnp.dot(
                    weights.astype(jnp.bfloat16), values[:end], preferred_element_type=jnp.float32
                )
                out = both[:, :VDIM] / both[:, VDIM:]
                spot = pl.ds(pl.multiple_of(p * PAIR_V + h * VDIM, 128), VDIM)
                r.outs[b * step : end, spot] = out.astype(jnp.bfloat16)
        for d in range(1, n_local):
            reply(p, d).start()
        keep(p).start()
        return carry

    lax.fori_loop(0, front, pair, 0)
    kv_far.columns()
    lax.fori_loop(front, pairs, pair, 0)

    each(1, chips, lambda d: back(d).wait())
    kept.wait()
    each(1, chips, lambda d: go(d).wait_send())
    lat_gather.finish()
    kv_near.finish()
    kv_far.finish()

    def shared_sent(n, carry):
        @pl.when(n != node)
        def _():
            share(n).wait_send()

        return carry

    lax.fori_loop(0, n_node, shared_sent, 0)

    def settle(p, carry):
        for d in range(1, n_local):
            reply(p, d).wait()
        keep(p).wait()
        return carry

    lax.fori_loop(0, pairs, settle, 0)


def finish_kernel(arrived, results, dense, attention, routed, sem):
    rows = arrived.shape[0] // 4
    copies = [
        pltpu.make_async_copy(
            arrived.at[pl.ds(i * rows, rows)], attention.at[pl.ds(i * rows, rows)], sem.at[i]
        )
        for i in range(4)
    ]
    for copy in copies:
        copy.start()
    chips = results.shape[0]
    weight = dense[...]
    high = weight.astype(jnp.bfloat16)
    rest = weight - high.astype(jnp.float32)
    middle = rest.astype(jnp.bfloat16)
    low = (rest - middle.astype(jnp.float32)).astype(jnp.bfloat16)
    width = results.shape[2] // 7
    for j in range(7):
        cols = slice(j * width, (j + 1) * width)
        rows = (
            results[:, :, cols]
            .astype(jnp.float32)
            .reshape(chips * CAP, width)
            .astype(jnp.bfloat16)
        )
        sums = [
            lax.dot_general(
                term, rows, (((0,), (0,)), ((), ())), preferred_element_type=jnp.float32
            )
            for term in (high, middle, low)
        ]
        routed[:, cols] = (sums[0] + sums[1] + sums[2]).astype(jnp.bfloat16)
    for copy in copies:
        copy.wait()


def shards(
    n_node,
    n_local,
    hidden,
    latent_weight,
    latent_gain,
    queries,
    kv_weight,
    expert_ids,
    route_weights,
    gate_proj,
    up_proj,
    down_proj,
):
    tokens, width = hidden.shape
    chips = n_node * n_local // 2
    nz = 4 if n_node % 4 == 0 else n_node
    ny = n_node // nz
    bf16, f32 = jnp.bfloat16, jnp.float32
    length = n_local * tokens

    freqs = 10000.0 ** (-2.0 * np.arange(ROPE // 2) / ROPE)
    angles = np.arange(length)[:, None] * freqs[None, :]
    cosine, sine = np.cos(angles), np.sin(angles)
    turns = jnp.asarray(np.concatenate([cosine, cosine, -sine, sine], axis=1), f32)

    half = latent_weight.shape[0] // 2
    total = latent_weight.shape[1]
    kv_rows, kv_cols = kv_weight.shape
    q_cols = queries.shape[1] // n_local
    pairs = kv_cols // PAIR_KV
    vmem, hbm = pl.BlockSpec(memory_space=pltpu.VMEM), pl.BlockSpec(memory_space=pl.ANY)
    dma = pltpu.SemaphoreType.DMA
    chain = max(nz - 1, 1)
    gather = [dma((chain,))] * 4 + [dma((nz, max(ny - 1, 1)))] * 2
    others = max(n_local - 1, 1)
    width_e = gate_proj.shape[2]
    operands = dict(
        hidden=hidden,
        ids=expert_ids.T,
        route_w=route_weights.T,
        gain=latent_gain.reshape(1, -1),
        turns=turns,
        latent_w=latent_weight,
        queries=queries,
        kv_w=kv_weight,
        gate_w=gate_proj,
        up_w=up_proj,
        down_w=down_proj,
    )
    scratch = dict(
        lat=pltpu.VMEM((n_node, 2, half, total), bf16),
        kv=pltpu.VMEM((n_node, kv_rows, kv_cols), bf16),
        q=pltpu.VMEM((n_local, tokens, q_cols), bf16),
        seq=pltpu.VMEM((n_local, tokens, total), bf16),
        outs=pltpu.VMEM((length, kv_cols // 2), bf16),
        gates=pltpu.VMEM((width, width_e), bf16),
        ups=pltpu.VMEM((width, width_e), bf16),
        downs=pltpu.VMEM((width_e, width), bf16),
        leaving=pltpu.VMEM((chips, CAP, width), bf16),
        arrived=pltpu.VMEM((2, chips, CAP, width), bf16),
        part=pltpu.VMEM((2, chips, CAP, width), bf16),
        sibpart=pltpu.VMEM((chips, CAP, width), bf16),
        mine=pltpu.VMEM((tokens, total), bf16),
        local_sem=dma((8,)),
        core_s=dma((n_node,)),
        core_r=dma((n_node,)),
        q_s=dma((others,)),
        q_r=dma((others,)),
        seq_s=dma((others,)),
        seq_r=dma((others,)),
        go_s=dma((chips - 1,)),
        go_r=dma((chips - 1,)),
        back_s=dma((chips - 1,)),
        back_r=dma((chips - 1,)),
        sib_s=dma((2,)),
        sib_r=dma((2,)),
        out_s=dma((pairs, others)),
        out_r=dma((pairs, others)),
        keep=dma((pairs,)),
    )
    names = [*operands, "attention", "results", "dense", *scratch]

    def body(*refs):
        r = types.SimpleNamespace(**dict(zip(names, refs)))
        rest = refs[len(names) :]
        r.lat_sems, r.near_sems, r.far_sems = rest[:6], rest[6:12], rest[12:]
        block_kernel(n_node, n_local, nz, EXPERTS // chips, r)

    attention, results, dense = pl.pallas_call(
        body,
        out_shape=(
            jax.ShapeDtypeStruct((tokens, n_local * kv_cols // 2), bf16),
            jax.ShapeDtypeStruct((chips, CAP, width), bf16),
            jax.ShapeDtypeStruct((chips * CAP, tokens), f32),
        ),
        in_specs=[vmem] * 5 + [hbm] * 6,
        out_specs=(hbm, hbm, vmem),
        scratch_shapes=[*scratch.values(), *gather * 3],
        compiler_params=pltpu.CompilerParams(
            collective_id=0, has_side_effects=True, vmem_limit_bytes=VMEM_LIMIT
        ),
        name="block",
    )(*operands.values())
    return pl.pallas_call(
        finish_kernel,
        out_shape=(
            jax.ShapeDtypeStruct(attention.shape, bf16),
            jax.ShapeDtypeStruct((tokens, width), bf16),
        ),
        in_specs=[hbm, vmem, vmem],
        out_specs=(hbm, vmem),
        scratch_shapes=[dma((4,))],
        compiler_params=pltpu.CompilerParams(vmem_limit_bytes=VMEM_LIMIT),
        name="finish",
    )(attention, results, dense)


def solution(mesh):
    placed = (
        P(("node", "local"), None),
        P("node", None),
        P(),
        P(("node", "local"), None),
        P("node", "local"),
        P(("node", "local"), None),
        P(("node", "local"), None),
        P(("node", "local"), None, None),
        P(("node", "local"), None, None),
        P(("node", "local"), None, None),
    )
    return jax.shard_map(
        functools.partial(shards, mesh.shape["node"], mesh.shape["local"]),
        mesh=mesh,
        in_specs=placed,
        out_specs=(P(("node", "local"), None), P(("node", "local"), None)),
        check_vma=False,
    )
```

```python
import functools
import math
import types

import jax
import jax.numpy as jnp
import numpy as np
from jax import lax
from jax.experimental import pallas as pl
from jax.experimental.pallas import tpu as pltpu
from jax.sharding import PartitionSpec as P

NOPE = 128
ROPE = 64
VDIM = 128
LAT = 512
EXPERTS = 256
CAP = 8
PAIR_Q = 2 * (NOPE + ROPE)
PAIR_KV = 2 * (NOPE + VDIM)
PAIR_V = 2 * VDIM
MESH = pl.DeviceIdType.MESH
VMEM_LIMIT = 56 * 2**20


def remote(src, dst, send_sem, recv_sem, device):
    return pltpu.make_async_remote_copy(
        src_ref=src,
        dst_ref=dst,
        send_sem=send_sem,
        recv_sem=recv_sem,
        device_id=device,
        device_id_type=MESH,
    )


def greet(devices, n_local, me):
    barrier = pltpu.get_barrier_semaphore()

    def signal(d, carry):
        other = lax.rem(me + d, devices)
        pl.semaphore_signal(
            barrier,
            inc=1,
            device_id=(lax.div(other, n_local), lax.rem(other, n_local)),
            device_id_type=MESH,
        )
        return carry

    lax.fori_loop(1, devices, signal, 0)
    pl.semaphore_wait(barrier, devices - 1)


class Gather:
    def __init__(self, own, slot, nz, ny, node, local, sems):
        self.own, self.slot, self.nz, self.ny = own, slot, nz, ny
        self.z, self.y, self.local = lax.div(node, ny), lax.rem(node, ny), local
        self.up_s, self.up_r, self.dn_s, self.dn_r, self.y_s, self.y_r = sems

    def up(self, h, src):
        z = jnp.maximum(self.z - h, 0)
        dst = self.slot(z * self.ny + self.y)
        to = jnp.minimum(self.z + 1, self.nz - 1)
        return remote(
            dst if src is None else src, dst, self.up_s.at[h], self.up_r.at[h], (to * self.ny + self.y, self.local)
        )

    def down(self, h, src):
        z = jnp.minimum(self.z + h, self.nz - 1)
        dst = self.slot(z * self.ny + self.y)
        to = jnp.maximum(self.z - 1, 0)
        return remote(
            dst if src is None else src, dst, self.dn_s.at[h], self.dn_r.at[h], (to * self.ny + self.y, self.local)
        )

    def across(self, z, dy, src):
        dst = self.slot(z * self.ny + self.y)
        to = self.z * self.ny + lax.rem(self.y + dy, self.ny)
        return remote(
            dst if src is None else src, dst, self.y_s.at[z, dy - 1], self.y_r.at[z, dy - 1], (to, self.local)
        )

    def begin(self):
        @pl.when(self.z < self.nz - 1)
        def _():
            self.up(0, self.own).start()

        @pl.when(self.z > 0)
        def _():
            self.down(0, self.own).start()

        for dy in range(1, self.ny):
            self.across(self.z, dy, self.own).start()

    def hop(self, h, landed=None):
        @pl.when(self.z - h >= 0)
        def _():
            self.up(h - 1, None).wait_recv()
            if h < self.nz - 1:

                @pl.when(self.z < self.nz - 1)
                def _():
                    self.up(h, None).start()

            for dy in range(1, self.ny):
                self.across(self.z - h, dy, None).start()
            if landed:
                landed((self.z - h) * self.ny + self.y)

        @pl.when(self.z + h < self.nz)
        def _():
            self.down(h - 1, None).wait_recv()
            if h < self.nz - 1:

                @pl.when(self.z > 0)
                def _():
                    self.down(h, None).start()

            for dy in range(1, self.ny):
                self.across(self.z + h, dy, None).start()
            if landed:
                landed((self.z + h) * self.ny + self.y)

    def columns(self, landed=None):
        for z in range(self.nz):
            for dy in range(1, self.ny):
                self.across(z, dy, None).wait_recv()
                if landed:
                    landed(z * self.ny + lax.rem(self.y - dy + self.ny, self.ny))

    def finish(self):
        for h in range(self.nz - 1):

            @pl.when((self.z < self.nz - 1) & (self.z - h >= 0))
            def _():
                self.up(h, None).wait_send()

            @pl.when((self.z > 0) & (self.z + h < self.nz))
            def _():
                self.down(h, None).wait_send()

        for z in range(self.nz):
            for dy in range(1, self.ny):
                self.across(z, dy, None).wait_send()


def present_routes(ids, gates, tokens, chips, stride):
    shape = (chips * CAP, tokens)
    row = lax.broadcasted_iota(jnp.int32, shape, 0)
    expert = lax.div(row, CAP) * stride
    count = jnp.zeros(shape, jnp.float32)
    weight = jnp.zeros(shape, jnp.float32)
    for k in range(ids.shape[0]):
        hit = ids[k : k + 1, :] == expert
        count += jnp.where(hit, 1.0, 0.0)
        weight += jnp.where(hit, gates[k : k + 1, :], 0.0)
    square = (tokens, tokens)
    earlier = lax.broadcasted_iota(jnp.int32, square, 0) < lax.broadcasted_iota(
        jnp.int32, square, 1
    )
    slot = jnp.dot(
        count.astype(jnp.bfloat16),
        jnp.where(earlier, 1.0, 0.0).astype(jnp.bfloat16),
        preferred_element_type=jnp.float32,
    )
    chosen = jnp.where(slot == lax.rem(row, CAP).astype(jnp.float32), count, 0.0)
    return chosen, chosen * weight


def block_kernel(n_node, n_local, nz, stride, r):
    node, local = lax.axis_index("node"), lax.axis_index("local")
    devices, ny = n_node * n_local, n_node // nz
    chips = devices // 2
    me = node * n_local + local
    chip, core = lax.div(me, 2), lax.rem(me, 2)
    sibling = (node, local + 1 - 2 * core)
    half = r.lat.shape[2]
    tokens = r.hidden.shape[0]
    q_cols = r.q.shape[2]
    length = n_local * tokens
    pairs = r.kv.shape[2] // PAIR_KV
    wide = r.kv.shape[2] // 2
    parts = len(r.kv_sems)
    front = pairs // parts

    own_q = pl.ds(pl.multiple_of(local * q_cols, 128), q_cols)
    weights_in = [
        pltpu.make_async_copy(r.gate_w.at[0], r.gates, r.local_sem.at[0]),
        pltpu.make_async_copy(r.up_w.at[0], r.ups, r.local_sem.at[1]),
        pltpu.make_async_copy(r.down_w.at[0], r.downs, r.local_sem.at[2]),
    ]
    kv_in = pltpu.make_async_copy(r.kv_w, r.kv.at[node], r.local_sem.at[3])
    q_in = pltpu.make_async_copy(r.queries.at[:, own_q], r.q.at[local], r.local_sem.at[4])
    lat_in = [
        pltpu.make_async_copy(
            r.latent_w.at[pl.ds(i * half, half)], r.lat.at[node, i], r.local_sem.at[5 + i]
        )
        for i in range(2)
    ]

    for copy in (*lat_in, kv_in, q_in, *weights_in):
        copy.start()

    chosen, dense = present_routes(r.ids, r.route_w, tokens, chips, stride)
    r.dense[...] = dense
    rows = jnp.dot(
        chosen.astype(jnp.bfloat16), r.hidden[...], preferred_element_type=jnp.float32
    )
    r.leaving[...] = rows.reshape(r.leaving.shape).astype(jnp.bfloat16)
    r.arrived[core * chips + chip] = r.leaving[chip]
    mine_blocks = pl.ds(core * chips, chips)

    greet(devices, n_local, me)

    def device_of(c):
        dev = c * 2 + core
        return (lax.div(dev, n_local), lax.rem(dev, n_local))

    def go(d):
        to = lax.rem(chip + d, chips)
        return remote(
            r.leaving.at[to],
            r.arrived.at[core * chips + chip],
            r.go_s.at[d - 1],
            r.go_r.at[d - 1],
            device_of(to),
        )

    def back(d):
        to = lax.rem(chip + d, chips)
        return remote(
            r.part.at[core * chips + to],
            r.results.at[chip],
            r.back_s.at[d - 1],
            r.back_r.at[d - 1],
            device_of(to),
        )

    def each(first, last, act):
        def step(d, carry):
            act(d)
            return carry

        lax.fori_loop(first, last, step, 0)

    def ask(d):
        to = lax.rem(local + d, n_local)
        cols = pl.ds(pl.multiple_of(to * q_cols, 128), q_cols)
        return remote(
            r.queries.at[:, cols], r.q.at[local], r.q_s.at[d - 1], r.q_r.at[d - 1], (node, to)
        )

    lat_gather = Gather(
        r.latent_w.at[pl.ds(pl.multiple_of(core * half, 16), half)],
        lambda n: r.lat.at[n, core],
        nz,
        ny,
        node,
        local,
        r.lat_sems,
    )
    def part_of_kv(i):
        cols = pl.ds(i * front * PAIR_KV, front * PAIR_KV)
        return Gather(
            r.kv_w.at[:, cols], lambda n: r.kv.at[n, :, cols], nz, ny, node, local, r.kv_sems[i]
        )

    kv_parts = [part_of_kv(i) for i in range(parts)]

    def share(n):
        return remote(
            r.lat.at[n, core], r.lat.at[n, core], r.core_s.at[n], r.core_r.at[n], sibling
        )

    def landed(n):
        share(n).start()

    def wave(step):
        if step < nz:
            lat_gather.hop(step, landed)
        for i, gather in enumerate(kv_parts):
            if step == i:
                gather.begin()
            elif 1 <= step - i < nz:
                gather.hop(step - i)

    waves = nz + parts - 1
    lat_gather.begin()
    each(1, chips, lambda d: go(d).start())
    kv_parts[0].begin()
    for d in range(1, n_local):
        ask(d).start()

    wave(1)
    each(1, chips, lambda d: go(d).wait_recv())
    swap = remote(
        r.arrived.at[mine_blocks], r.arrived.at[mine_blocks], r.sib_s.at[0], r.sib_r.at[0], sibling
    )
    swap.start()
    wave(2)
    for copy in weights_in:
        copy.wait()
    swap.wait()
    batch = min(32, 2 * chips)

    def expert(i, carry):
        at = pl.ds(i * batch, batch)
        x = r.arrived[at].astype(jnp.float32).reshape(batch * CAP, -1).astype(jnp.bfloat16)
        gate = jnp.dot(x, r.gates[...], preferred_element_type=jnp.float32)
        upper = jnp.dot(x, r.ups[...], preferred_element_type=jnp.float32)
        inner = (gate / (1.0 + jnp.exp(-gate)) * upper).astype(jnp.bfloat16)
        width = r.downs.shape[1] // 7
        for j in range(7):
            cols = slice(j * width, (j + 1) * width)
            y = jnp.dot(inner, r.downs[:, cols], preferred_element_type=jnp.float32)
            r.part[at, :, cols] = y.reshape(batch, CAP, width).astype(jnp.bfloat16)
        return carry

    lax.fori_loop(0, 2 * chips // batch, expert, 0)
    give = remote(
        r.part.at[pl.ds((1 - core) * chips, chips)],
        r.sibpart,
        r.sib_s.at[1],
        r.sib_r.at[1],
        sibling,
    )
    give.start()
    wave(3)

    lat_gather.columns(landed)

    def shared(n, carry):
        @pl.when(n != node)
        def _():
            remote(
                r.lat.at[n, 1 - core],
                r.lat.at[n, 1 - core],
                r.core_s.at[n],
                r.core_r.at[n],
                sibling,
            ).wait_recv()

        return carry

    lax.fori_loop(0, n_node, shared, 0)
    for copy in lat_in:
        copy.wait()
    weight = r.lat[...].reshape(n_node * 2 * half, r.lat.shape[3])
    latent = jnp.dot(r.hidden[...], weight, preferred_element_type=jnp.float32)
    u = latent[:, :LAT]
    norm = lax.rsqrt(jnp.mean(u * u, axis=1, keepdims=True) + 1e-06)
    r.mine[:, :LAT] = (u * norm * r.gain[...]).astype(jnp.bfloat16)
    a = latent[:, LAT:]
    swapped = jnp.concatenate([a[:, ROPE // 2 :], a[:, : ROPE // 2]], axis=1)
    turn = r.turns[pl.ds(pl.multiple_of(local * tokens, 16), tokens)]
    r.mine[:, LAT:] = (a * turn[:, :ROPE] + swapped * turn[:, ROPE:]).astype(jnp.bfloat16)

    def tell(d):
        to = lax.rem(local + d, n_local)
        return remote(
            r.mine, r.seq.at[local], r.seq_s.at[d - 1], r.seq_r.at[d - 1], (node, to)
        )

    for d in range(1, n_local):
        tell(d).start()
    r.seq[local] = r.mine[...]

    wave(4)
    give.wait()

    def total(p, carry):
        at = core * chips + p
        both = r.part[at].astype(jnp.float32) + r.sibpart[p].astype(jnp.float32)
        r.part[at] = both.astype(jnp.bfloat16)
        return carry

    lax.fori_loop(0, chips, total, 0)
    kept = pltpu.make_async_copy(
        r.part.at[core * chips + chip], r.results.at[chip], r.local_sem.at[7]
    )
    kept.start()

    kv_in.wait()
    q_in.wait()
    for d in range(1, n_local):
        ask(d).wait()
        tell(d).wait()

    scale = math.log2(math.e) / math.sqrt(NOPE + ROPE)
    step = 256
    diagonal = lax.broadcasted_iota(jnp.int32, (step, step), 1) <= lax.broadcasted_iota(
        jnp.int32, (step, step), 0
    )

    def place(p):
        return pl.ds(pl.multiple_of(local * wide + p * PAIR_V, 128), PAIR_V)

    def out_cols(p):
        return pl.ds(pl.multiple_of(p * PAIR_V, 128), PAIR_V)

    def reply(p, d):
        to = lax.rem(local + d, n_local)
        rows = pl.ds(pl.multiple_of(to * tokens, 16), tokens)
        return remote(
            r.outs.at[rows, out_cols(p)],
            r.attention.at[:, place(p)],
            r.out_s.at[p, d - 1],
            r.out_r.at[p, d - 1],
            (node, to),
        )

    def keep(p):
        rows = pl.ds(pl.multiple_of(local * tokens, 16), tokens)
        return pltpu.make_async_copy(
            r.outs.at[rows, out_cols(p)], r.attention.at[:, place(p)], r.keep.at[p]
        )

    def pair(p, carry):
        cols = pl.ds(pl.multiple_of(p * PAIR_KV, 128), PAIR_KV)
        compressed = r.seq[:, :, :LAT].reshape(length, LAT)
        rope = r.seq[:, :, LAT:].reshape(length, ROPE).astype(jnp.float32)
        zeros = jnp.zeros((length, 128 - ROPE), jnp.float32)
        ones = jnp.ones((length, VDIM), jnp.bfloat16)
        up = r.kv[:, :, cols].reshape(LAT, PAIR_KV)
        keyval = jnp.dot(compressed, up, preferred_element_type=jnp.float32)
        first = jnp.concatenate([keyval[:, :NOPE], rope, zeros], axis=1).astype(jnp.bfloat16)
        at = NOPE + VDIM
        second = jnp.concatenate([zeros, keyval[:, at : at + NOPE], rope], axis=1).astype(
            jnp.bfloat16
        )
        for h, keys in enumerate((first, second)):
            values = jnp.concatenate(
                [keyval[:, h * at + NOPE : (h + 1) * at].astype(jnp.bfloat16), ones], axis=1
            )
            window = pl.ds(pl.multiple_of(p * PAIR_Q + h * 128, 128), 256)
            asked = r.q[:, :, window].reshape(length, 256)
            for b in range(length // step):
                end = (b + 1) * step
                scores = lax.dot_general(
                    asked[b * step : end],
                    keys[:end],
                    (((1,), (1,)), ((), ())),
                    preferred_element_type=jnp.float32,
                )
                last = jnp.where(diagonal, scores[:, b * step :], -1e30)
                scores = jnp.concatenate([scores[:, : b * step], last], axis=1) if b else last
                weights = jnp.exp2((scores - jnp.max(scores, axis=1, keepdims=True)) * scale)
                both = jnp.dot(
                    weights.astype(jnp.bfloat16), values[:end], preferred_element_type=jnp.float32
                )
                out = both[:, :VDIM] / both[:, VDIM:]
                spot = pl.ds(pl.multiple_of(p * PAIR_V + h * VDIM, 128), VDIM)
                r.outs[b * step : end, spot] = out.astype(jnp.bfloat16)
        for d in range(1, n_local):
            reply(p, d).start()
        keep(p).start()
        return carry

    for i in range(parts):
        kv_parts[i].columns()
        lax.fori_loop(i * front, (i + 1) * front, pair, 0)
        if i + 5 < waves:
            wave(i + 5)
        if i == 0:
            each(1, chips, lambda d: back(d).start())

    each(1, chips, lambda d: back(d).wait())
    kept.wait()
    each(1, chips, lambda d: go(d).wait_send())
    lat_gather.finish()
    for gather in kv_parts:
        gather.finish()

    def shared_sent(n, carry):
        @pl.when(n != node)
        def _():
            share(n).wait_send()

        return carry

    lax.fori_loop(0, n_node, shared_sent, 0)

    def settle(p, carry):
        for d in range(1, n_local):
            reply(p, d).wait()
        keep(p).wait()
        return carry

    lax.fori_loop(0, pairs, settle, 0)


def finish_kernel(arrived, results, dense, attention, routed):
    attention[...] = arrived[...]
    chips = results.shape[0]
    weight = dense[...]
    high = weight.astype(jnp.bfloat16)
    rest = weight - high.astype(jnp.float32)
    middle = rest.astype(jnp.bfloat16)
    low = (rest - middle.astype(jnp.float32)).astype(jnp.bfloat16)
    rows = (
        results[...].astype(jnp.float32).reshape(chips * CAP, -1).astype(jnp.bfloat16)
    )
    sums = [
        lax.dot_general(term, rows, (((0,), (0,)), ((), ())), preferred_element_type=jnp.float32)
        for term in (high, middle, low)
    ]
    routed[...] = (sums[0] + sums[1] + sums[2]).astype(jnp.bfloat16)


def shards(
    n_node,
    n_local,
    hidden,
    latent_weight,
    latent_gain,
    queries,
    kv_weight,
    expert_ids,
    route_weights,
    gate_proj,
    up_proj,
    down_proj,
):
    tokens, width = hidden.shape
    chips = n_node * n_local // 2
    nz = 4 if n_node % 4 == 0 else n_node
    ny = n_node // nz
    bf16, f32 = jnp.bfloat16, jnp.float32
    length = n_local * tokens

    freqs = 10000.0 ** (-2.0 * np.arange(ROPE // 2) / ROPE)
    angles = np.arange(length)[:, None] * freqs[None, :]
    cosine, sine = np.cos(angles), np.sin(angles)
    turns = jnp.asarray(np.concatenate([cosine, cosine, -sine, sine], axis=1), f32)

    half = latent_weight.shape[0] // 2
    total = latent_weight.shape[1]
    kv_rows, kv_cols = kv_weight.shape
    q_cols = queries.shape[1] // n_local
    pairs = kv_cols // PAIR_KV
    vmem, hbm = pl.BlockSpec(memory_space=pltpu.VMEM), pl.BlockSpec(memory_space=pl.ANY)
    dma = pltpu.SemaphoreType.DMA
    chain = max(nz - 1, 1)
    gather = [dma((chain,))] * 4 + [dma((nz, max(ny - 1, 1)))] * 2
    others = max(n_local - 1, 1)
    width_e = gate_proj.shape[2]
    operands = dict(
        hidden=hidden,
        ids=expert_ids.T,
        route_w=route_weights.T,
        gain=latent_gain.reshape(1, -1),
        turns=turns,
        latent_w=latent_weight,
        queries=queries,
        kv_w=kv_weight,
        gate_w=gate_proj,
        up_w=up_proj,
        down_w=down_proj,
    )
    scratch = dict(
        lat=pltpu.VMEM((n_node, 2, half, total), bf16),
        kv=pltpu.VMEM((n_node, kv_rows, kv_cols), bf16),
        q=pltpu.VMEM((n_local, tokens, q_cols), bf16),
        seq=pltpu.VMEM((n_local, tokens, total), bf16),
        outs=pltpu.VMEM((length, kv_cols // 2), bf16),
        gates=pltpu.VMEM((width, width_e), bf16),
        ups=pltpu.VMEM((width, width_e), bf16),
        downs=pltpu.VMEM((width_e, width), bf16),
        leaving=pltpu.VMEM((chips, CAP, width), bf16),
        arrived=pltpu.VMEM((2 * chips, CAP, width), bf16),
        part=pltpu.VMEM((2 * chips, CAP, width), bf16),
        sibpart=pltpu.VMEM((chips, CAP, width), bf16),
        mine=pltpu.VMEM((tokens, total), bf16),
        local_sem=dma((8,)),
        core_s=dma((n_node,)),
        core_r=dma((n_node,)),
        q_s=dma((others,)),
        q_r=dma((others,)),
        seq_s=dma((others,)),
        seq_r=dma((others,)),
        go_s=dma((chips - 1,)),
        go_r=dma((chips - 1,)),
        back_s=dma((chips - 1,)),
        back_r=dma((chips - 1,)),
        sib_s=dma((2,)),
        sib_r=dma((2,)),
        out_s=dma((pairs, others)),
        out_r=dma((pairs, others)),
        keep=dma((pairs,)),
    )
    names = [*operands, "attention", "results", "dense", *scratch]

    def body(*refs):
        r = types.SimpleNamespace(**dict(zip(names, refs)))
        rest = refs[len(names) :]
        r.lat_sems = rest[:6]
        r.kv_sems = [rest[i : i + 6] for i in range(6, len(rest), 6)]
        block_kernel(n_node, n_local, nz, EXPERTS // chips, r)

    attention, results, dense = pl.pallas_call(
        body,
        out_shape=(
            jax.ShapeDtypeStruct((tokens, n_local * kv_cols // 2), bf16),
            jax.ShapeDtypeStruct((chips, CAP, width), bf16),
            jax.ShapeDtypeStruct((chips * CAP, tokens), f32),
        ),
        in_specs=[vmem] * 5 + [hbm] * 6,
        out_specs=(hbm, hbm, vmem),
        scratch_shapes=[*scratch.values(), *gather * (1 + min(4, pairs))],
        compiler_params=pltpu.CompilerParams(
            collective_id=0, has_side_effects=True, vmem_limit_bytes=VMEM_LIMIT
        ),
        name="block",
    )(*operands.values())
    steps = 4
    return pl.pallas_call(
        finish_kernel,
        out_shape=(
            jax.ShapeDtypeStruct(attention.shape, bf16),
            jax.ShapeDtypeStruct((tokens, width), bf16),
        ),
        grid=(steps,),
        in_specs=[
            pl.BlockSpec((tokens, attention.shape[1] // steps), lambda i: (0, i)),
            pl.BlockSpec((chips, CAP, width // steps), lambda i: (0, 0, i)),
            pl.BlockSpec(dense.shape, lambda i: (0, 0)),
        ],
        out_specs=(
            pl.BlockSpec((tokens, attention.shape[1] // steps), lambda i: (0, i)),
            pl.BlockSpec((tokens, width // steps), lambda i: (0, i)),
        ),
        compiler_params=pltpu.CompilerParams(vmem_limit_bytes=VMEM_LIMIT),
        name="finish",
    )(attention, results, dense)


def solution(mesh):
    placed = (
        P(("node", "local"), None),
        P("node", None),
        P(),
        P(("node", "local"), None),
        P("node", "local"),
        P(("node", "local"), None),
        P(("node", "local"), None),
        P(("node", "local"), None, None),
        P(("node", "local"), None, None),
        P(("node", "local"), None, None),
    )
    return jax.shard_map(
        functools.partial(shards, mesh.shape["node"], mesh.shape["local"]),
        mesh=mesh,
        in_specs=placed,
        out_specs=(P(("node", "local"), None), P(("node", "local"), None)),
        check_vma=False,
    )
```

```python
import functools
import math
import types

import jax
import jax.numpy as jnp
import numpy as np
from jax import lax
from jax.experimental import pallas as pl
from jax.experimental.pallas import tpu as pltpu
from jax.sharding import PartitionSpec as P

NOPE = 128
ROPE = 64
VDIM = 128
LAT = 512
EXPERTS = 256
CAP = 8
PAIR_Q = 2 * (NOPE + ROPE)
PAIR_KV = 2 * (NOPE + VDIM)
PAIR_V = 2 * VDIM
MESH = pl.DeviceIdType.MESH
VMEM_LIMIT = 56 * 2**20


def remote(src, dst, send_sem, recv_sem, device):
    return pltpu.make_async_remote_copy(
        src_ref=src,
        dst_ref=dst,
        send_sem=send_sem,
        recv_sem=recv_sem,
        device_id=device,
        device_id_type=MESH,
    )


def greet(devices, n_local, me):
    barrier = pltpu.get_barrier_semaphore()

    def signal(d, carry):
        other = lax.rem(me + d, devices)
        pl.semaphore_signal(
            barrier,
            inc=1,
            device_id=(lax.div(other, n_local), lax.rem(other, n_local)),
            device_id_type=MESH,
        )
        return carry

    lax.fori_loop(1, devices, signal, 0)
    pl.semaphore_wait(barrier, devices - 1)


class Gather:
    def __init__(self, own, slot, nz, ny, node, local, sems):
        self.own, self.slot, self.nz, self.ny = own, slot, nz, ny
        self.z, self.y, self.local = lax.div(node, ny), lax.rem(node, ny), local
        self.up_s, self.up_r, self.dn_s, self.dn_r, self.y_s, self.y_r = sems

    def up(self, h, src):
        z = jnp.maximum(self.z - h, 0)
        dst = self.slot(z * self.ny + self.y)
        to = jnp.minimum(self.z + 1, self.nz - 1)
        return remote(
            dst if src is None else src, dst, self.up_s.at[h], self.up_r.at[h], (to * self.ny + self.y, self.local)
        )

    def down(self, h, src):
        z = jnp.minimum(self.z + h, self.nz - 1)
        dst = self.slot(z * self.ny + self.y)
        to = jnp.maximum(self.z - 1, 0)
        return remote(
            dst if src is None else src, dst, self.dn_s.at[h], self.dn_r.at[h], (to * self.ny + self.y, self.local)
        )

    def across(self, z, dy, src):
        dst = self.slot(z * self.ny + self.y)
        to = self.z * self.ny + lax.rem(self.y + dy, self.ny)
        return remote(
            dst if src is None else src, dst, self.y_s.at[z, dy - 1], self.y_r.at[z, dy - 1], (to, self.local)
        )

    def begin(self):
        @pl.when(self.z < self.nz - 1)
        def _():
            self.up(0, self.own).start()

        @pl.when(self.z > 0)
        def _():
            self.down(0, self.own).start()

        for dy in range(1, self.ny):
            self.across(self.z, dy, self.own).start()

    def hop(self, h, landed=None):
        @pl.when(self.z - h >= 0)
        def _():
            self.up(h - 1, None).wait_recv()
            if h < self.nz - 1:

                @pl.when(self.z < self.nz - 1)
                def _():
                    self.up(h, None).start()

            for dy in range(1, self.ny):
                self.across(self.z - h, dy, None).start()
            if landed:
                landed((self.z - h) * self.ny + self.y)

        @pl.when(self.z + h < self.nz)
        def _():
            self.down(h - 1, None).wait_recv()
            if h < self.nz - 1:

                @pl.when(self.z > 0)
                def _():
                    self.down(h, None).start()

            for dy in range(1, self.ny):
                self.across(self.z + h, dy, None).start()
            if landed:
                landed((self.z + h) * self.ny + self.y)

    def columns(self, landed=None):
        for z in range(self.nz):
            for dy in range(1, self.ny):
                self.across(z, dy, None).wait_recv()
                if landed:
                    landed(z * self.ny + lax.rem(self.y - dy + self.ny, self.ny))

    def finish(self):
        for h in range(self.nz - 1):

            @pl.when((self.z < self.nz - 1) & (self.z - h >= 0))
            def _():
                self.up(h, None).wait_send()

            @pl.when((self.z > 0) & (self.z + h < self.nz))
            def _():
                self.down(h, None).wait_send()

        for z in range(self.nz):
            for dy in range(1, self.ny):
                self.across(z, dy, None).wait_send()


def present_routes(ids, gates, tokens, chips, stride):
    shape = (chips * CAP, tokens)
    row = lax.broadcasted_iota(jnp.int32, shape, 0)
    expert = lax.div(row, CAP) * stride
    count = jnp.zeros(shape, jnp.float32)
    weight = jnp.zeros(shape, jnp.float32)
    for k in range(ids.shape[0]):
        hit = ids[k : k + 1, :] == expert
        count += jnp.where(hit, 1.0, 0.0)
        weight += jnp.where(hit, gates[k : k + 1, :], 0.0)
    square = (tokens, tokens)
    earlier = lax.broadcasted_iota(jnp.int32, square, 0) < lax.broadcasted_iota(
        jnp.int32, square, 1
    )
    slot = jnp.dot(
        count.astype(jnp.bfloat16),
        jnp.where(earlier, 1.0, 0.0).astype(jnp.bfloat16),
        preferred_element_type=jnp.float32,
    )
    chosen = jnp.where(slot == lax.rem(row, CAP).astype(jnp.float32), count, 0.0)
    return chosen, chosen * weight


def block_kernel(n_node, n_local, nz, stride, r):
    node, local = lax.axis_index("node"), lax.axis_index("local")
    devices, ny = n_node * n_local, n_node // nz
    chips = devices // 2
    me = node * n_local + local
    chip, core = lax.div(me, 2), lax.rem(me, 2)
    sibling = (node, local + 1 - 2 * core)
    half = r.lat.shape[2]
    tokens = r.hidden.shape[0]
    q_cols = r.q.shape[2]
    length = n_local * tokens
    pairs = r.kv.shape[2] // PAIR_KV
    wide = r.kv.shape[2] // 2
    parts = len(r.kv_sems)
    front = pairs // parts

    own_q = pl.ds(pl.multiple_of(local * q_cols, 128), q_cols)
    weights_in = [
        pltpu.make_async_copy(r.gate_w.at[0], r.gates, r.local_sem.at[0]),
        pltpu.make_async_copy(r.up_w.at[0], r.ups, r.local_sem.at[1]),
        pltpu.make_async_copy(r.down_w.at[0], r.downs, r.local_sem.at[2]),
    ]
    kv_in = pltpu.make_async_copy(r.kv_w, r.kv.at[node], r.local_sem.at[3])
    q_in = pltpu.make_async_copy(r.queries.at[:, own_q], r.q.at[local], r.local_sem.at[4])
    lat_in = [
        pltpu.make_async_copy(
            r.latent_w.at[pl.ds(i * half, half)], r.lat.at[node, i], r.local_sem.at[5 + i]
        )
        for i in range(2)
    ]

    for copy in (*lat_in, kv_in, q_in, *weights_in):
        copy.start()

    greet(devices, n_local, me)

    def device_of(c):
        dev = c * 2 + core
        return (lax.div(dev, n_local), lax.rem(dev, n_local))

    def go(d):
        to = lax.rem(chip + d, chips)
        return remote(
            r.leaving.at[to],
            r.arrived.at[core * chips + chip],
            r.go_s.at[d - 1],
            r.go_r.at[d - 1],
            device_of(to),
        )

    def back(d):
        to = lax.rem(chip + d, chips)
        return remote(
            r.part.at[core * chips + to],
            r.results.at[chip],
            r.back_s.at[d - 1],
            r.back_r.at[d - 1],
            device_of(to),
        )

    def each(first, last, act):
        def step(d, carry):
            act(d)
            return carry

        lax.fori_loop(first, last, step, 0)

    def ask(d):
        to = lax.rem(local + d, n_local)
        cols = pl.ds(pl.multiple_of(to * q_cols, 128), q_cols)
        return remote(
            r.queries.at[:, cols], r.q.at[local], r.q_s.at[d - 1], r.q_r.at[d - 1], (node, to)
        )

    lat_gather = Gather(
        r.latent_w.at[pl.ds(pl.multiple_of(core * half, 16), half)],
        lambda n: r.lat.at[n, core],
        nz,
        ny,
        node,
        local,
        r.lat_sems,
    )
    def part_of_kv(i):
        cols = pl.ds(i * front * PAIR_KV, front * PAIR_KV)
        return Gather(
            r.kv_w.at[:, cols], lambda n: r.kv.at[n, :, cols], nz, ny, node, local, r.kv_sems[i]
        )

    kv_parts = [part_of_kv(i) for i in range(parts)]
    later = [0 if 2 * i < parts else 1 for i in range(parts)]
    mine_blocks = pl.ds(core * chips, chips)

    def share(n):
        return remote(
            r.lat.at[n, core], r.lat.at[n, core], r.core_s.at[n], r.core_r.at[n], sibling
        )

    def landed(n):
        share(n).start()

    def wave(step):
        if step < nz:
            lat_gather.hop(step, landed)
        for i, gather in enumerate(kv_parts):
            if step == later[i]:
                gather.begin()
            elif 1 <= step - later[i] < nz:
                gather.hop(step - later[i])

    lat_gather.begin()
    for i in range(parts):
        if later[i] == 0:
            kv_parts[i].begin()
    for d in range(1, n_local):
        ask(d).start()

    chosen, dense = present_routes(r.ids, r.route_w, tokens, chips, stride)
    slots = chips * CAP
    same = lax.broadcasted_iota(jnp.int32, (slots, slots), 0) == lax.broadcasted_iota(
        jnp.int32, (slots, slots), 1
    )
    unit = jnp.where(same, 1.0, 0.0).astype(jnp.bfloat16)
    for i in range(3):
        term = dense.astype(jnp.bfloat16)
        dense = dense - term.astype(jnp.float32)
        turned = lax.dot_general(
            term, unit, (((0,), (0,)), ((), ())), preferred_element_type=jnp.float32
        )
        r.terms[:, i * slots : (i + 1) * slots] = turned.astype(jnp.bfloat16)
    rows = jnp.dot(
        chosen.astype(jnp.bfloat16), r.hidden[...], preferred_element_type=jnp.float32
    )
    r.leaving[...] = rows.reshape(r.leaving.shape).astype(jnp.bfloat16)
    r.arrived[core * chips + chip] = r.leaving[chip]

    each(1, chips, lambda d: go(d).start())

    wave(1)
    each(1, chips, lambda d: go(d).wait_recv())
    swap = remote(
        r.arrived.at[mine_blocks], r.arrived.at[mine_blocks], r.sib_s.at[0], r.sib_r.at[0], sibling
    )
    swap.start()
    wave(2)
    for copy in weights_in:
        copy.wait()
    swap.wait()
    batch = min(32, 2 * chips)

    def expert(i, carry):
        at = pl.ds(i * batch, batch)
        x = r.arrived[at].astype(jnp.float32).reshape(batch * CAP, -1).astype(jnp.bfloat16)
        gate = jnp.dot(x, r.gates[...], preferred_element_type=jnp.float32)
        upper = jnp.dot(x, r.ups[...], preferred_element_type=jnp.float32)
        inner = (gate / (1.0 + jnp.exp(-gate)) * upper).astype(jnp.bfloat16)
        width = r.downs.shape[1] // 7
        for j in range(7):
            cols = slice(j * width, (j + 1) * width)
            y = jnp.dot(inner, r.downs[:, cols], preferred_element_type=jnp.float32)
            r.part[at, :, cols] = y.reshape(batch, CAP, width).astype(jnp.bfloat16)
        return carry

    lax.fori_loop(0, 2 * chips // batch, expert, 0)
    give = remote(
        r.part.at[pl.ds((1 - core) * chips, chips)],
        r.sibpart,
        r.sib_s.at[1],
        r.sib_r.at[1],
        sibling,
    )
    give.start()
    wave(3)

    lat_gather.columns(landed)

    def shared(n, carry):
        @pl.when(n != node)
        def _():
            remote(
                r.lat.at[n, 1 - core],
                r.lat.at[n, 1 - core],
                r.core_s.at[n],
                r.core_r.at[n],
                sibling,
            ).wait_recv()

        return carry

    lax.fori_loop(0, n_node, shared, 0)
    for copy in lat_in:
        copy.wait()
    weight = r.lat[...].reshape(n_node * 2 * half, r.lat.shape[3])
    latent = jnp.dot(r.hidden[...], weight, preferred_element_type=jnp.float32)
    u = latent[:, :LAT]
    norm = lax.rsqrt(jnp.mean(u * u, axis=1, keepdims=True) + 1e-06)
    r.mine[:, :LAT] = (u * norm * r.gain[...]).astype(jnp.bfloat16)
    a = latent[:, LAT:]
    swapped = jnp.concatenate([a[:, ROPE // 2 :], a[:, : ROPE // 2]], axis=1)
    turn = r.turns[pl.ds(pl.multiple_of(local * tokens, 16), tokens)]
    r.mine[:, LAT:] = (a * turn[:, :ROPE] + swapped * turn[:, ROPE:]).astype(jnp.bfloat16)

    def tell(d):
        to = lax.rem(local + d, n_local)
        return remote(
            r.mine, r.seq.at[local], r.seq_s.at[d - 1], r.seq_r.at[d - 1], (node, to)
        )

    for d in range(1, n_local):
        tell(d).start()
    r.seq[local] = r.mine[...]

    wave(4)
    give.wait()

    def total(p, carry):
        at = core * chips + p
        both = r.part[at].astype(jnp.float32) + r.sibpart[p].astype(jnp.float32)
        r.part[at] = both.astype(jnp.bfloat16)
        return carry

    lax.fori_loop(0, chips, total, 0)
    kept = pltpu.make_async_copy(
        r.part.at[core * chips + chip], r.results.at[chip], r.local_sem.at[7]
    )
    kept.start()
    each(1, chips, lambda d: back(d).start())

    kv_in.wait()
    q_in.wait()
    for d in range(1, n_local):
        ask(d).wait()
        tell(d).wait()

    scale = math.log2(math.e) / math.sqrt(NOPE + ROPE)
    step = 256
    diagonal = lax.broadcasted_iota(jnp.int32, (step, step), 1) <= lax.broadcasted_iota(
        jnp.int32, (step, step), 0
    )

    def place(p):
        return pl.ds(pl.multiple_of(local * wide + p * PAIR_V, 128), PAIR_V)

    def out_cols(p):
        return pl.ds(pl.multiple_of(p * PAIR_V, 128), PAIR_V)

    def reply(p, d):
        to = lax.rem(local + d, n_local)
        rows = pl.ds(pl.multiple_of(to * tokens, 16), tokens)
        return remote(
            r.outs.at[rows, out_cols(p)],
            r.attention.at[:, place(p)],
            r.out_s.at[p, d - 1],
            r.out_r.at[p, d - 1],
            (node, to),
        )

    def keep(p):
        rows = pl.ds(pl.multiple_of(local * tokens, 16), tokens)
        return pltpu.make_async_copy(
            r.outs.at[rows, out_cols(p)], r.attention.at[:, place(p)], r.keep.at[p]
        )

    def pair(p, carry):
        cols = pl.ds(pl.multiple_of(p * PAIR_KV, 128), PAIR_KV)
        compressed = r.seq[:, :, :LAT].reshape(length, LAT)
        rope = r.seq[:, :, LAT:].reshape(length, ROPE).astype(jnp.float32)
        zeros = jnp.zeros((length, 128 - ROPE), jnp.float32)
        ones = jnp.ones((length, VDIM), jnp.bfloat16)
        up = r.kv[:, :, cols].reshape(LAT, PAIR_KV)
        keyval = jnp.dot(compressed, up, preferred_element_type=jnp.float32)
        first = jnp.concatenate([keyval[:, :NOPE], rope, zeros], axis=1).astype(jnp.bfloat16)
        at = NOPE + VDIM
        second = jnp.concatenate([zeros, keyval[:, at : at + NOPE], rope], axis=1).astype(
            jnp.bfloat16
        )
        for h, keys in enumerate((first, second)):
            values = jnp.concatenate(
                [keyval[:, h * at + NOPE : (h + 1) * at].astype(jnp.bfloat16), ones], axis=1
            )
            window = pl.ds(pl.multiple_of(p * PAIR_Q + h * 128, 128), 256)
            asked = r.q[:, :, window].reshape(length, 256)
            for b in range(length // step):
                end = (b + 1) * step
                scores = lax.dot_general(
                    asked[b * step : end],
                    keys[:end],
                    (((1,), (1,)), ((), ())),
                    preferred_element_type=jnp.float32,
                )
                last = jnp.where(diagonal, scores[:, b * step :], -1e30)
                scores = jnp.concatenate([scores[:, : b * step], last], axis=1) if b else last
                weights = jnp.exp2((scores - jnp.max(scores, axis=1, keepdims=True)) * scale)
                both = jnp.dot(
                    weights.astype(jnp.bfloat16), values[:end], preferred_element_type=jnp.float32
                )
                out = both[:, :VDIM] / both[:, VDIM:]
                spot = pl.ds(pl.multiple_of(p * PAIR_V + h * VDIM, 128), VDIM)
                r.outs[b * step : end, spot] = out.astype(jnp.bfloat16)
        for d in range(1, n_local):
            reply(p, d).start()
        keep(p).start()
        return carry

    for i in range(parts):
        kv_parts[i].columns()
        lax.fori_loop(i * front, (i + 1) * front, pair, 0)

    each(1, chips, lambda d: back(d).wait())
    kept.wait()
    each(1, chips, lambda d: go(d).wait_send())
    lat_gather.finish()
    for gather in kv_parts:
        gather.finish()

    def shared_sent(n, carry):
        @pl.when(n != node)
        def _():
            share(n).wait_send()

        return carry

    lax.fori_loop(0, n_node, shared_sent, 0)

    def settle(p, carry):
        for d in range(1, n_local):
            reply(p, d).wait()
        keep(p).wait()
        return carry

    lax.fori_loop(0, pairs, settle, 0)


def finish_kernel(arrived, results, terms, attention, routed):
    attention[...] = arrived[...]
    chips = results.shape[0]
    rows = (
        results[...].astype(jnp.float32).reshape(chips * CAP, -1).astype(jnp.bfloat16)
    )
    slots = chips * CAP
    total = jnp.zeros(routed.shape, jnp.float32)
    for i in range(3):
        total += jnp.dot(
            terms[:, i * slots : (i + 1) * slots], rows, preferred_element_type=jnp.float32
        )
    routed[...] = total.astype(jnp.bfloat16)


def shards(
    n_node,
    n_local,
    hidden,
    latent_weight,
    latent_gain,
    queries,
    kv_weight,
    expert_ids,
    route_weights,
    gate_proj,
    up_proj,
    down_proj,
):
    tokens, width = hidden.shape
    chips = n_node * n_local // 2
    nz = 4 if n_node % 4 == 0 else n_node
    ny = n_node // nz
    bf16, f32 = jnp.bfloat16, jnp.float32
    length = n_local * tokens

    freqs = 10000.0 ** (-2.0 * np.arange(ROPE // 2) / ROPE)
    angles = np.arange(length)[:, None] * freqs[None, :]
    cosine, sine = np.cos(angles), np.sin(angles)
    turns = jnp.asarray(np.concatenate([cosine, cosine, -sine, sine], axis=1), f32)

    half = latent_weight.shape[0] // 2
    total = latent_weight.shape[1]
    kv_rows, kv_cols = kv_weight.shape
    q_cols = queries.shape[1] // n_local
    pairs = kv_cols // PAIR_KV
    vmem, hbm = pl.BlockSpec(memory_space=pltpu.VMEM), pl.BlockSpec(memory_space=pl.ANY)
    dma = pltpu.SemaphoreType.DMA
    chain = max(nz - 1, 1)
    gather = [dma((chain,))] * 4 + [dma((nz, max(ny - 1, 1)))] * 2
    others = max(n_local - 1, 1)
    width_e = gate_proj.shape[2]
    operands = dict(
        hidden=hidden,
        ids=expert_ids.T,
        route_w=route_weights.T,
        gain=latent_gain.reshape(1, -1),
        turns=turns,
        latent_w=latent_weight,
        queries=queries,
        kv_w=kv_weight,
        gate_w=gate_proj,
        up_w=up_proj,
        down_w=down_proj,
    )
    scratch = dict(
        lat=pltpu.VMEM((n_node, 2, half, total), bf16),
        kv=pltpu.VMEM((n_node, kv_rows, kv_cols), bf16),
        q=pltpu.VMEM((n_local, tokens, q_cols), bf16),
        seq=pltpu.VMEM((n_local, tokens, total), bf16),
        outs=pltpu.VMEM((length, kv_cols // 2), bf16),
        gates=pltpu.VMEM((width, width_e), bf16),
        ups=pltpu.VMEM((width, width_e), bf16),
        downs=pltpu.VMEM((width_e, width), bf16),
        leaving=pltpu.VMEM((chips, CAP, width), bf16),
        arrived=pltpu.VMEM((2 * chips, CAP, width), bf16),
        part=pltpu.VMEM((2 * chips, CAP, width), bf16),
        sibpart=pltpu.VMEM((chips, CAP, width), bf16),
        mine=pltpu.VMEM((tokens, total), bf16),
        local_sem=dma((8,)),
        core_s=dma((n_node,)),
        core_r=dma((n_node,)),
        q_s=dma((others,)),
        q_r=dma((others,)),
        seq_s=dma((others,)),
        seq_r=dma((others,)),
        go_s=dma((chips - 1,)),
        go_r=dma((chips - 1,)),
        back_s=dma((chips - 1,)),
        back_r=dma((chips - 1,)),
        sib_s=dma((2,)),
        sib_r=dma((2,)),
        out_s=dma((pairs, others)),
        out_r=dma((pairs, others)),
        keep=dma((pairs,)),
    )
    names = [*operands, "attention", "results", "terms", *scratch]

    def body(*refs):
        r = types.SimpleNamespace(**dict(zip(names, refs)))
        rest = refs[len(names) :]
        r.lat_sems = rest[:6]
        r.kv_sems = [rest[i : i + 6] for i in range(6, len(rest), 6)]
        block_kernel(n_node, n_local, nz, EXPERTS // chips, r)

    attention, results, terms = pl.pallas_call(
        body,
        out_shape=(
            jax.ShapeDtypeStruct((tokens, n_local * kv_cols // 2), bf16),
            jax.ShapeDtypeStruct((chips, CAP, width), bf16),
            jax.ShapeDtypeStruct((tokens, 3 * chips * CAP), bf16),
        ),
        in_specs=[vmem] * 5 + [hbm] * 6,
        out_specs=(hbm, hbm, vmem),
        scratch_shapes=[*scratch.values(), *gather * (1 + min(4, pairs))],
        compiler_params=pltpu.CompilerParams(
            collective_id=0, has_side_effects=True, vmem_limit_bytes=VMEM_LIMIT
        ),
        name="block",
    )(*operands.values())
    steps = 4
    return pl.pallas_call(
        finish_kernel,
        out_shape=(
            jax.ShapeDtypeStruct(attention.shape, bf16),
            jax.ShapeDtypeStruct((tokens, width), bf16),
        ),
        grid=(steps,),
        in_specs=[
            pl.BlockSpec((tokens, attention.shape[1] // steps), lambda i: (0, i)),
            pl.BlockSpec((chips, CAP, width // steps), lambda i: (0, 0, i)),
            pl.BlockSpec(terms.shape, lambda i: (0, 0)),
        ],
        out_specs=(
            pl.BlockSpec((tokens, attention.shape[1] // steps), lambda i: (0, i)),
            pl.BlockSpec((tokens, width // steps), lambda i: (0, i)),
        ),
        compiler_params=pltpu.CompilerParams(vmem_limit_bytes=VMEM_LIMIT),
        name="finish",
    )(attention, results, terms)


def solution(mesh):
    placed = (
        P(("node", "local"), None),
        P("node", None),
        P(),
        P(("node", "local"), None),
        P("node", "local"),
        P(("node", "local"), None),
        P(("node", "local"), None),
        P(("node", "local"), None, None),
        P(("node", "local"), None, None),
        P(("node", "local"), None, None),
    )
    return jax.shard_map(
        functools.partial(shards, mesh.shape["node"], mesh.shape["local"]),
        mesh=mesh,
        in_specs=placed,
        out_specs=(P(("node", "local"), None), P(("node", "local"), None)),
        check_vma=False,
    )
```

```python
import functools
import math
import types

import jax
import jax.numpy as jnp
import numpy as np
from jax import lax
from jax.experimental import pallas as pl
from jax.experimental.pallas import tpu as pltpu
from jax.sharding import PartitionSpec as P

NOPE = 128
ROPE = 64
VDIM = 128
LAT = 512
EXPERTS = 256
CAP = 8
PAIR_Q = 2 * (NOPE + ROPE)
PAIR_KV = 2 * (NOPE + VDIM)
PAIR_V = 2 * VDIM
MESH = pl.DeviceIdType.MESH
VMEM_LIMIT = 56 * 2**20


def remote(src, dst, send_sem, recv_sem, device):
    return pltpu.make_async_remote_copy(
        src_ref=src,
        dst_ref=dst,
        send_sem=send_sem,
        recv_sem=recv_sem,
        device_id=device,
        device_id_type=MESH,
    )


def greet(devices, n_local, me):
    barrier = pltpu.get_barrier_semaphore()

    def signal(d, carry):
        other = lax.rem(me + d, devices)
        pl.semaphore_signal(
            barrier,
            inc=1,
            device_id=(lax.div(other, n_local), lax.rem(other, n_local)),
            device_id_type=MESH,
        )
        return carry

    lax.fori_loop(1, devices, signal, 0)
    pl.semaphore_wait(barrier, devices - 1)


class Gather:
    def __init__(self, own, slot, nz, ny, node, local, sems):
        self.own, self.slot, self.nz, self.ny = own, slot, nz, ny
        self.z, self.y, self.local = lax.div(node, ny), lax.rem(node, ny), local
        self.up_s, self.up_r, self.dn_s, self.dn_r, self.y_s, self.y_r = sems

    def up(self, h, src):
        z = jnp.maximum(self.z - h, 0)
        dst = self.slot(z * self.ny + self.y)
        to = jnp.minimum(self.z + 1, self.nz - 1)
        return remote(
            dst if src is None else src, dst, self.up_s.at[h], self.up_r.at[h], (to * self.ny + self.y, self.local)
        )

    def down(self, h, src):
        z = jnp.minimum(self.z + h, self.nz - 1)
        dst = self.slot(z * self.ny + self.y)
        to = jnp.maximum(self.z - 1, 0)
        return remote(
            dst if src is None else src, dst, self.dn_s.at[h], self.dn_r.at[h], (to * self.ny + self.y, self.local)
        )

    def across(self, z, dy, src):
        dst = self.slot(z * self.ny + self.y)
        to = self.z * self.ny + lax.rem(self.y + dy, self.ny)
        return remote(
            dst if src is None else src, dst, self.y_s.at[z, dy - 1], self.y_r.at[z, dy - 1], (to, self.local)
        )

    def begin(self):
        @pl.when(self.z < self.nz - 1)
        def _():
            self.up(0, self.own).start()

        @pl.when(self.z > 0)
        def _():
            self.down(0, self.own).start()

        for dy in range(1, self.ny):
            self.across(self.z, dy, self.own).start()

    def hop(self, h, landed=None):
        @pl.when(self.z - h >= 0)
        def _():
            self.up(h - 1, None).wait_recv()
            if h < self.nz - 1:

                @pl.when(self.z < self.nz - 1)
                def _():
                    self.up(h, None).start()

            for dy in range(1, self.ny):
                self.across(self.z - h, dy, None).start()
            if landed:
                landed((self.z - h) * self.ny + self.y)

        @pl.when(self.z + h < self.nz)
        def _():
            self.down(h - 1, None).wait_recv()
            if h < self.nz - 1:

                @pl.when(self.z > 0)
                def _():
                    self.down(h, None).start()

            for dy in range(1, self.ny):
                self.across(self.z + h, dy, None).start()
            if landed:
                landed((self.z + h) * self.ny + self.y)

    def columns(self, landed=None):
        for z in range(self.nz):
            for dy in range(1, self.ny):
                self.across(z, dy, None).wait_recv()
                if landed:
                    landed(z * self.ny + lax.rem(self.y - dy + self.ny, self.ny))

    def finish(self):
        for h in range(self.nz - 1):

            @pl.when((self.z < self.nz - 1) & (self.z - h >= 0))
            def _():
                self.up(h, None).wait_send()

            @pl.when((self.z > 0) & (self.z + h < self.nz))
            def _():
                self.down(h, None).wait_send()

        for z in range(self.nz):
            for dy in range(1, self.ny):
                self.across(z, dy, None).wait_send()


def present_routes(ids, gates, tokens, chips, stride):
    shape = (chips * CAP, tokens)
    row = lax.broadcasted_iota(jnp.int32, shape, 0)
    expert = lax.div(row, CAP) * stride
    count = jnp.zeros(shape, jnp.float32)
    weight = jnp.zeros(shape, jnp.float32)
    for k in range(ids.shape[0]):
        hit = ids[k : k + 1, :] == expert
        count += jnp.where(hit, 1.0, 0.0)
        weight += jnp.where(hit, gates[k : k + 1, :], 0.0)
    square = (tokens, tokens)
    earlier = lax.broadcasted_iota(jnp.int32, square, 0) < lax.broadcasted_iota(
        jnp.int32, square, 1
    )
    slot = jnp.dot(
        count.astype(jnp.bfloat16),
        jnp.where(earlier, 1.0, 0.0).astype(jnp.bfloat16),
        preferred_element_type=jnp.float32,
    )
    chosen = jnp.where(slot == lax.rem(row, CAP).astype(jnp.float32), count, 0.0)
    return chosen, chosen * weight


def block_kernel(n_node, n_local, nz, stride, r):
    node, local = lax.axis_index("node"), lax.axis_index("local")
    devices, ny = n_node * n_local, n_node // nz
    chips = devices // 2
    me = node * n_local + local
    chip, core = lax.div(me, 2), lax.rem(me, 2)
    sibling = (node, local + 1 - 2 * core)
    half = r.lat.shape[2]
    tokens = r.hidden.shape[0]
    q_cols = r.q.shape[2]
    length = n_local * tokens
    pairs = r.kv.shape[2] // PAIR_KV
    wide = r.kv.shape[2] // 2
    parts = len(r.kv_sems)
    front = pairs // parts

    own_q = pl.ds(pl.multiple_of(local * q_cols, 128), q_cols)
    weights_in = [
        pltpu.make_async_copy(r.gate_w.at[0], r.gates, r.local_sem.at[0]),
        pltpu.make_async_copy(r.up_w.at[0], r.ups, r.local_sem.at[1]),
        pltpu.make_async_copy(r.down_w.at[0], r.downs, r.local_sem.at[2]),
    ]
    kv_in = pltpu.make_async_copy(r.kv_w, r.kv.at[node], r.local_sem.at[3])
    q_in = pltpu.make_async_copy(r.queries.at[:, own_q], r.q.at[local], r.local_sem.at[4])
    lat_in = [
        pltpu.make_async_copy(
            r.latent_w.at[pl.ds(i * half, half)], r.lat.at[node, i], r.local_sem.at[5 + i]
        )
        for i in range(2)
    ]

    for copy in (*lat_in, kv_in, q_in, *weights_in):
        copy.start()

    mine_blocks = pl.ds(core * chips, chips)
    greet(devices, n_local, me)

    def device_of(c):
        dev = c * 2 + core
        return (lax.div(dev, n_local), lax.rem(dev, n_local))

    def go(d):
        to = lax.rem(chip + d, chips)
        return remote(
            r.leaving.at[to],
            r.arrived.at[core * chips + chip],
            r.go_s.at[d - 1],
            r.go_r.at[d - 1],
            device_of(to),
        )

    def back(d):
        to = lax.rem(chip + d, chips)
        return remote(
            r.part.at[core * chips + to],
            r.results.at[chip],
            r.back_s.at[d - 1],
            r.back_r.at[d - 1],
            device_of(to),
        )

    def each(first, last, act):
        def step(d, carry):
            act(d)
            return carry

        lax.fori_loop(first, last, step, 0)

    def ask(d):
        to = lax.rem(local + d, n_local)
        cols = pl.ds(pl.multiple_of(to * q_cols, 128), q_cols)
        return remote(
            r.queries.at[:, cols], r.q.at[local], r.q_s.at[d - 1], r.q_r.at[d - 1], (node, to)
        )

    lat_gather = Gather(
        r.latent_w.at[pl.ds(pl.multiple_of(core * half, 16), half)],
        lambda n: r.lat.at[n, core],
        nz,
        ny,
        node,
        local,
        r.lat_sems,
    )
    def part_of_kv(i):
        cols = pl.ds(i * front * PAIR_KV, front * PAIR_KV)
        return Gather(
            r.kv_w.at[:, cols], lambda n: r.kv.at[n, :, cols], nz, ny, node, local, r.kv_sems[i]
        )

    kv_parts = [part_of_kv(i) for i in range(parts)]

    def share(n):
        return remote(
            r.lat.at[n, core], r.lat.at[n, core], r.core_s.at[n], r.core_r.at[n], sibling
        )

    def landed(n):
        share(n).start()

    def wave(step):
        if step < nz:
            lat_gather.hop(step, landed)
        for i, gather in enumerate(kv_parts):
            if step == i:
                gather.begin()
            elif 1 <= step - i < nz:
                gather.hop(step - i)

    waves = nz + parts - 1
    lat_gather.begin()

    chosen, dense = present_routes(r.ids, r.route_w, tokens, chips, stride)
    r.dense[...] = dense
    rows = jnp.dot(
        chosen.astype(jnp.bfloat16), r.hidden[...], preferred_element_type=jnp.float32
    )
    r.leaving[...] = rows.reshape(r.leaving.shape).astype(jnp.bfloat16)
    r.arrived[core * chips + chip] = r.leaving[chip]

    each(1, chips, lambda d: go(d).start())
    kv_parts[0].begin()
    for d in range(1, n_local):
        ask(d).start()

    wave(1)
    each(1, chips, lambda d: go(d).wait_recv())
    swap = remote(
        r.arrived.at[mine_blocks], r.arrived.at[mine_blocks], r.sib_s.at[0], r.sib_r.at[0], sibling
    )
    swap.start()
    wave(2)
    for copy in weights_in:
        copy.wait()
    swap.wait()
    batch = min(32, 2 * chips)

    def expert(i, carry):
        at = pl.ds(i * batch, batch)
        x = r.arrived[at].astype(jnp.float32).reshape(batch * CAP, -1).astype(jnp.bfloat16)
        gate = jnp.dot(x, r.gates[...], preferred_element_type=jnp.float32)
        upper = jnp.dot(x, r.ups[...], preferred_element_type=jnp.float32)
        inner = (gate / (1.0 + jnp.exp(-gate)) * upper).astype(jnp.bfloat16)
        width = r.downs.shape[1] // 7
        for j in range(7):
            cols = slice(j * width, (j + 1) * width)
            y = jnp.dot(inner, r.downs[:, cols], preferred_element_type=jnp.float32)
            r.part[at, :, cols] = y.reshape(batch, CAP, width).astype(jnp.bfloat16)
        return carry

    lax.fori_loop(0, 2 * chips // batch, expert, 0)
    give = remote(
        r.part.at[pl.ds((1 - core) * chips, chips)],
        r.sibpart,
        r.sib_s.at[1],
        r.sib_r.at[1],
        sibling,
    )
    give.start()
    wave(3)

    lat_gather.columns(landed)

    def shared(n, carry):
        @pl.when(n != node)
        def _():
            remote(
                r.lat.at[n, 1 - core],
                r.lat.at[n, 1 - core],
                r.core_s.at[n],
                r.core_r.at[n],
                sibling,
            ).wait_recv()

        return carry

    lax.fori_loop(0, n_node, shared, 0)
    for copy in lat_in:
        copy.wait()
    weight = r.lat[...].reshape(n_node * 2 * half, r.lat.shape[3])
    latent = jnp.dot(r.hidden[...], weight, preferred_element_type=jnp.float32)
    u = latent[:, :LAT]
    norm = lax.rsqrt(jnp.mean(u * u, axis=1, keepdims=True) + 1e-06)
    r.mine[:, :LAT] = (u * norm * r.gain[...]).astype(jnp.bfloat16)
    a = latent[:, LAT:]
    swapped = jnp.concatenate([a[:, ROPE // 2 :], a[:, : ROPE // 2]], axis=1)
    turn = r.turns[pl.ds(pl.multiple_of(local * tokens, 16), tokens)]
    r.mine[:, LAT:] = (a * turn[:, :ROPE] + swapped * turn[:, ROPE:]).astype(jnp.bfloat16)

    def tell(d):
        to = lax.rem(local + d, n_local)
        return remote(
            r.mine, r.seq.at[local], r.seq_s.at[d - 1], r.seq_r.at[d - 1], (node, to)
        )

    for d in range(1, n_local):
        tell(d).start()
    r.seq[local] = r.mine[...]

    wave(4)
    give.wait()

    def total(p, carry):
        at = core * chips + p
        both = r.part[at].astype(jnp.float32) + r.sibpart[p].astype(jnp.float32)
        r.part[at] = both.astype(jnp.bfloat16)
        return carry

    lax.fori_loop(0, chips, total, 0)
    kept = pltpu.make_async_copy(
        r.part.at[core * chips + chip], r.results.at[chip], r.local_sem.at[7]
    )
    kept.start()

    kv_in.wait()
    q_in.wait()
    for d in range(1, n_local):
        ask(d).wait()
        tell(d).wait()

    scale = math.log2(math.e) / math.sqrt(NOPE + ROPE)
    step = 256
    diagonal = lax.broadcasted_iota(jnp.int32, (step, step), 1) <= lax.broadcasted_iota(
        jnp.int32, (step, step), 0
    )

    def place(p):
        return pl.ds(pl.multiple_of(local * wide + p * PAIR_V, 128), PAIR_V)

    def out_cols(p):
        return pl.ds(pl.multiple_of(p * PAIR_V, 128), PAIR_V)

    def reply(p, d):
        to = lax.rem(local + d, n_local)
        rows = pl.ds(pl.multiple_of(to * tokens, 16), tokens)
        return remote(
            r.outs.at[rows, out_cols(p)],
            r.attention.at[:, place(p)],
            r.out_s.at[p, d - 1],
            r.out_r.at[p, d - 1],
            (node, to),
        )

    def keep(p):
        rows = pl.ds(pl.multiple_of(local * tokens, 16), tokens)
        return pltpu.make_async_copy(
            r.outs.at[rows, out_cols(p)], r.attention.at[:, place(p)], r.keep.at[p]
        )

    def pair(p, carry):
        cols = pl.ds(pl.multiple_of(p * PAIR_KV, 128), PAIR_KV)
        compressed = r.seq[:, :, :LAT].reshape(length, LAT)
        rope = r.seq[:, :, LAT:].reshape(length, ROPE).astype(jnp.float32)
        zeros = jnp.zeros((length, 128 - ROPE), jnp.float32)
        ones = jnp.ones((length, VDIM), jnp.bfloat16)
        up = r.kv[:, :, cols].reshape(LAT, PAIR_KV)
        keyval = jnp.dot(compressed, up, preferred_element_type=jnp.float32)
        first = jnp.concatenate([keyval[:, :NOPE], rope, zeros], axis=1).astype(jnp.bfloat16)
        at = NOPE + VDIM
        second = jnp.concatenate([zeros, keyval[:, at : at + NOPE], rope], axis=1).astype(
            jnp.bfloat16
        )
        for h, keys in enumerate((first, second)):
            values = jnp.concatenate(
                [keyval[:, h * at + NOPE : (h + 1) * at].astype(jnp.bfloat16), ones], axis=1
            )
            window = pl.ds(pl.multiple_of(p * PAIR_Q + h * 128, 128), 256)
            asked = r.q[:, :, window].reshape(length, 256)
            for b in range(length // step):
                end = (b + 1) * step
                scores = lax.dot_general(
                    asked[b * step : end],
                    keys[:end],
                    (((1,), (1,)), ((), ())),
                    preferred_element_type=jnp.float32,
                )
                last = jnp.where(diagonal, scores[:, b * step :], -1e30)
                scores = jnp.concatenate([scores[:, : b * step], last], axis=1) if b else last
                weights = jnp.exp2((scores - jnp.max(scores, axis=1, keepdims=True)) * scale)
                both = jnp.dot(
                    weights.astype(jnp.bfloat16), values[:end], preferred_element_type=jnp.float32
                )
                out = both[:, :VDIM] / both[:, VDIM:]
                spot = pl.ds(pl.multiple_of(p * PAIR_V + h * VDIM, 128), VDIM)
                r.outs[b * step : end, spot] = out.astype(jnp.bfloat16)
        for d in range(1, n_local):
            reply(p, d).start()
        keep(p).start()
        return carry

    for i in range(parts):
        kv_parts[i].columns()
        lax.fori_loop(i * front, (i + 1) * front, pair, 0)
        if i + 5 < waves:
            wave(i + 5)
        if i == 0:
            each(1, chips, lambda d: back(d).start())

    each(1, chips, lambda d: back(d).wait())
    kept.wait()
    each(1, chips, lambda d: go(d).wait_send())
    lat_gather.finish()
    for gather in kv_parts:
        gather.finish()

    def shared_sent(n, carry):
        @pl.when(n != node)
        def _():
            share(n).wait_send()

        return carry

    lax.fori_loop(0, n_node, shared_sent, 0)

    def settle(p, carry):
        for d in range(1, n_local):
            reply(p, d).wait()
        keep(p).wait()
        return carry

    lax.fori_loop(0, pairs, settle, 0)


def finish_kernel(arrived, results, dense, attention, routed):
    attention[...] = arrived[...]
    chips = results.shape[0]
    weight = dense[...]
    high = weight.astype(jnp.bfloat16)
    rest = weight - high.astype(jnp.float32)
    middle = rest.astype(jnp.bfloat16)
    low = (rest - middle.astype(jnp.float32)).astype(jnp.bfloat16)
    rows = (
        results[...].astype(jnp.float32).reshape(chips * CAP, -1).astype(jnp.bfloat16)
    )
    sums = [
        lax.dot_general(term, rows, (((0,), (0,)), ((), ())), preferred_element_type=jnp.float32)
        for term in (high, middle, low)
    ]
    routed[...] = (sums[0] + sums[1] + sums[2]).astype(jnp.bfloat16)


def shards(
    n_node,
    n_local,
    hidden,
    latent_weight,
    latent_gain,
    queries,
    kv_weight,
    expert_ids,
    route_weights,
    gate_proj,
    up_proj,
    down_proj,
):
    tokens, width = hidden.shape
    chips = n_node * n_local // 2
    nz = 4 if n_node % 4 == 0 else n_node
    ny = n_node // nz
    bf16, f32 = jnp.bfloat16, jnp.float32
    length = n_local * tokens

    freqs = 10000.0 ** (-2.0 * np.arange(ROPE // 2) / ROPE)
    angles = np.arange(length)[:, None] * freqs[None, :]
    cosine, sine = np.cos(angles), np.sin(angles)
    turns = jnp.asarray(np.concatenate([cosine, cosine, -sine, sine], axis=1), f32)

    half = latent_weight.shape[0] // 2
    total = latent_weight.shape[1]
    kv_rows, kv_cols = kv_weight.shape
    q_cols = queries.shape[1] // n_local
    pairs = kv_cols // PAIR_KV
    vmem, hbm = pl.BlockSpec(memory_space=pltpu.VMEM), pl.BlockSpec(memory_space=pl.ANY)
    dma = pltpu.SemaphoreType.DMA
    chain = max(nz - 1, 1)
    gather = [dma((chain,))] * 4 + [dma((nz, max(ny - 1, 1)))] * 2
    others = max(n_local - 1, 1)
    width_e = gate_proj.shape[2]
    operands = dict(
        hidden=hidden,
        ids=expert_ids.T,
        route_w=route_weights.T,
        gain=latent_gain.reshape(1, -1),
        turns=turns,
        latent_w=latent_weight,
        queries=queries,
        kv_w=kv_weight,
        gate_w=gate_proj,
        up_w=up_proj,
        down_w=down_proj,
    )
    scratch = dict(
        lat=pltpu.VMEM((n_node, 2, half, total), bf16),
        kv=pltpu.VMEM((n_node, kv_rows, kv_cols), bf16),
        q=pltpu.VMEM((n_local, tokens, q_cols), bf16),
        seq=pltpu.VMEM((n_local, tokens, total), bf16),
        outs=pltpu.VMEM((length, kv_cols // 2), bf16),
        gates=pltpu.VMEM((width, width_e), bf16),
        ups=pltpu.VMEM((width, width_e), bf16),
        downs=pltpu.VMEM((width_e, width), bf16),
        leaving=pltpu.VMEM((chips, CAP, width), bf16),
        arrived=pltpu.VMEM((2 * chips, CAP, width), bf16),
        part=pltpu.VMEM((2 * chips, CAP, width), bf16),
        sibpart=pltpu.VMEM((chips, CAP, width), bf16),
        mine=pltpu.VMEM((tokens, total), bf16),
        local_sem=dma((8,)),
        core_s=dma((n_node,)),
        core_r=dma((n_node,)),
        q_s=dma((others,)),
        q_r=dma((others,)),
        seq_s=dma((others,)),
        seq_r=dma((others,)),
        go_s=dma((chips - 1,)),
        go_r=dma((chips - 1,)),
        back_s=dma((chips - 1,)),
        back_r=dma((chips - 1,)),
        sib_s=dma((2,)),
        sib_r=dma((2,)),
        out_s=dma((pairs, others)),
        out_r=dma((pairs, others)),
        keep=dma((pairs,)),
    )
    names = [*operands, "attention", "results", "dense", *scratch]

    def body(*refs):
        r = types.SimpleNamespace(**dict(zip(names, refs)))
        rest = refs[len(names) :]
        r.lat_sems = rest[:6]
        r.kv_sems = [rest[i : i + 6] for i in range(6, len(rest), 6)]
        block_kernel(n_node, n_local, nz, EXPERTS // chips, r)

    attention, results, dense = pl.pallas_call(
        body,
        out_shape=(
            jax.ShapeDtypeStruct((tokens, n_local * kv_cols // 2), bf16),
            jax.ShapeDtypeStruct((chips, CAP, width), bf16),
            jax.ShapeDtypeStruct((chips * CAP, tokens), f32),
        ),
        in_specs=[vmem] * 5 + [hbm] * 6,
        out_specs=(hbm, hbm, vmem),
        scratch_shapes=[*scratch.values(), *gather * (1 + min(4, pairs))],
        compiler_params=pltpu.CompilerParams(
            collective_id=0, has_side_effects=True, vmem_limit_bytes=VMEM_LIMIT
        ),
        name="block",
    )(*operands.values())
    steps = 4
    return pl.pallas_call(
        finish_kernel,
        out_shape=(
            jax.ShapeDtypeStruct(attention.shape, bf16),
            jax.ShapeDtypeStruct((tokens, width), bf16),
        ),
        grid=(steps,),
        in_specs=[
            pl.BlockSpec((tokens, attention.shape[1] // steps), lambda i: (0, i)),
            pl.BlockSpec((chips, CAP, width // steps), lambda i: (0, 0, i)),
            pl.BlockSpec(dense.shape, lambda i: (0, 0)),
        ],
        out_specs=(
            pl.BlockSpec((tokens, attention.shape[1] // steps), lambda i: (0, i)),
            pl.BlockSpec((tokens, width // steps), lambda i: (0, i)),
        ),
        compiler_params=pltpu.CompilerParams(vmem_limit_bytes=VMEM_LIMIT),
        name="finish",
    )(attention, results, dense)


def solution(mesh):
    placed = (
        P(("node", "local"), None),
        P("node", None),
        P(),
        P(("node", "local"), None),
        P("node", "local"),
        P(("node", "local"), None),
        P(("node", "local"), None),
        P(("node", "local"), None, None),
        P(("node", "local"), None, None),
        P(("node", "local"), None, None),
    )
    return jax.shard_map(
        functools.partial(shards, mesh.shape["node"], mesh.shape["local"]),
        mesh=mesh,
        in_specs=placed,
        out_specs=(P(("node", "local"), None), P(("node", "local"), None)),
        check_vma=False,
    )
```
